768 devices in a mesh: blk: 8 (over x, y_lo), grp: 96 (over y_hi, z, core).
Axes of the slice: x: 4, y: 8 (y_hi: 4, y_lo: 2; y = y_hi * 2 + y_lo), z: 12, core: 2. Of those that a mesh axis runs over, the one named last changes fastest.
Arguments:
- features: bfloat16 [1572864, 128], P(('blk', 'grp')), may hold values from -6 to 6
- send_rows: int32 [8, 96, 8], P('blk', 'grp'), may hold values from 0 to 2047
- tile_rows: int32 [8, 96, 32], P('blk', 'grp'), may hold values from 0 to 15
- tile_cols: int32 [8, 96, 32], P('blk', 'grp'), may hold values from 0 to 47
- tile_vals: bfloat16 [8, 96, 32, 128, 128], P('blk', 'grp'), may hold values from -0.375 to 0.375
- w_self: bfloat16 [128, 256], replicated, may hold values from -0.5 to 0.5
- w_neigh: bfloat16 [128, 256], replicated, may hold values from -0.5 to 0.5
- bias: float32 [256], replicated, may hold values from -4 to 4
- grad_out: bfloat16 [1572864, 256], P(('blk', 'grp')), may hold values from -6 to 6
Outputs:
- activations: bfloat16 [1572864, 256], P(('blk', 'grp'))
- grad_self: float32 [128, 256], replicated
- grad_neigh: float32 [128, 256], replicated
The draws below stay inside these ranges and needn't reach their ends.
All inputs are finite; a program needn't handle non-finite values.
Results may differ from the reference program's by a relative error of at most 0.015.
Values may be sent and summed in bfloat16 or wider, within the bound.
A program may use at most 32 MiB of HBM per device.

```python
import jax
import jax.numpy as jnp
from jax import lax

F_IN = 128
HID = 256
BS = 128
SEND = 8
ROWS_DEV = 2048
TILES = 32
NODES = 1572864
RB = 16
NPB = 48
N_BLK = 8
N_GRP = 96


def set_ends(array, rng, smallest, largest):
    place = [jax.random.randint(jax.random.fold_in(rng, axis), (), 0, length) for axis, length in enumerate(array.shape)]
    widest = array.shape.index(max(array.shape))
    next_to = place[:widest] + [(place[widest] + 1) % array.shape[widest]] + place[widest + 1:]
    return array.at[tuple(place)].set(smallest).at[tuple(next_to)].set(largest)


def block_levels(stream_key, extent, split, smallest, high):
    factor_of = 1.0
    for position, shards_of in split:
        heights = jax.random.uniform(jax.random.fold_in(jax.random.fold_in(stream_key, 6), position), (shards_of,), jnp.float32, smallest / len(split), high / len(split))
        factor_of = factor_of * jnp.repeat(jnp.exp(heights), extent[position] // shards_of).reshape((-1,) + (1,) * (len(extent) - 1 - position))
    return factor_of


def gaussian(own_key, shape, deviation, limit, shards=(), kind=jnp.bfloat16):
    gain = block_levels(own_key, shape, shards, -0.22, 0.18) if shards else 1.0
    values = jax.random.normal(own_key, shape, jnp.float32) * deviation * gain
    return jnp.minimum(jnp.maximum(values, -limit), limit).astype(kind)


def setup_inputs(seed: int = 0) -> dict:
    keys = jax.random.split(jax.random.key(seed), 10)
    features = gaussian(keys[0], (NODES, F_IN), 1.0, 6.0, ((0, 768),))
    send_rows = set_ends(jax.random.randint(keys[1], (N_BLK, N_GRP, SEND), 0, ROWS_DEV), jax.random.fold_in(keys[1], 1), 0, ROWS_DEV - 1).astype(jnp.int32)
    tile_rows = set_ends(jax.random.randint(keys[2], (N_BLK, N_GRP, TILES), 0, RB), jax.random.fold_in(keys[2], 1), 0, RB - 1).astype(jnp.int32)
    tile_cols = set_ends(jax.random.randint(keys[3], (N_BLK, N_GRP, TILES), 0, NPB), jax.random.fold_in(keys[3], 1), 0, NPB - 1).astype(jnp.int32)
    tile_vals = gaussian(keys[4], (N_BLK, N_GRP, TILES, BS, BS), (BS * TILES // RB) ** -0.5, 0.375, ((0, 8), (1, 96)))
    w_self = gaussian(keys[5], (F_IN, HID), F_IN ** -0.5, 0.5)
    w_neigh = gaussian(keys[6], (F_IN, HID), F_IN ** -0.5, 0.5)
    bias = gaussian(keys[7], (HID,), 1.0, 4.0, (), jnp.float32)
    grad_out = gaussian(keys[8], (NODES, HID), 1.0, 6.0, ((0, 768),))
    return {"features": features, "send_rows": send_rows, "tile_rows": tile_rows, "tile_cols": tile_cols, "tile_vals": tile_vals, "w_self": w_self, "w_neigh": w_neigh, "bias": bias, "grad_out": grad_out}


def reference(features, send_rows, tile_rows, tile_cols, tile_vals, w_self, w_neigh, bias, grad_out):
    ndev = N_BLK * N_GRP
    xdev = features.reshape(ndev, ROWS_DEV, F_IN)
    sends = send_rows.reshape(ndev, SEND).astype(jnp.int32)
    shared = jnp.take_along_axis(xdev, sends[:, :, None], axis=1).reshape(-1, BS, F_IN)
    rows = tile_rows.reshape(ndev, TILES)
    cols = tile_cols.reshape(ndev, TILES)
    vals = tile_vals.reshape(ndev, TILES, BS, BS)
    blocks = jnp.arange(ROWS_DEV // BS, dtype=jnp.int32)

    def one_device(packed):
        row_ids, col_ids, entries = packed
        taken = shared[col_ids].astype(jnp.float32)
        product = jnp.einsum('tij,tjf->tif', entries.astype(jnp.float32), taken)
        onehot = (row_ids[:, None] == blocks[None, :]).astype(jnp.float32)
        return jnp.einsum('tr,tif->rif', onehot, product).reshape(ROWS_DEV, F_IN)
    neigh = lax.map(one_device, (rows, cols, vals)).reshape(-1, F_IN).astype(jnp.bfloat16)
    pre = jnp.dot(features, w_self, preferred_element_type=jnp.float32)
    pre = pre + jnp.dot(neigh, w_neigh, preferred_element_type=jnp.float32) + bias
    sig = jax.nn.sigmoid(pre)
    activations = (pre * sig).astype(jnp.bfloat16)
    grad_pre = (grad_out.astype(jnp.float32) * sig * (1.0 + pre * (1.0 - sig))).astype(jnp.bfloat16)
    factor = 1.0 / jnp.sqrt(jnp.float32(NODES))
    grad_self = jnp.dot(features.T, grad_pre, preferred_element_type=jnp.float32) * factor
    grad_neigh = jnp.dot(neigh.T, grad_pre, preferred_element_type=jnp.float32) * factor
    return (activations, grad_self, grad_neigh)
```

```python
import functools

import jax
import jax.numpy as jnp
from jax import lax
from jax.experimental import pallas as pl
from jax.experimental.pallas import tpu as pltpu
from jax.sharding import PartitionSpec as P

MESH = pl.DeviceIdType.MESH
BS = 128
F_IN = 128
HID = 256
SEND = 8
NX = 4
YLO = 2


def ring_order(n):
    return sorted(range(1, n), key=lambda k: (min(k, n - k), k))


def kernel(
    dims,
    send_rows, tile_rows, tile_cols,
    feat_hbm, vals_hbm, ws_hbm, wn_hbm, bias_ref, gout_hbm,
    act_hbm, gs_ref, gn_ref,
    xn, w, vals, gout, act, gp, zbuf, mine, shared, prods, links,
    part, rx_core, half, rx_x, slab, rx_y, tile, rx_z, final,
    load_sem, out_sem,
    zs, zr, ys, yr, xs, xr, rs, rr, cs, cr,
    r0, r1, rxs, rxr, rys, ryr, rzs, rzr, fys, fyr, fxs, fxr, fcs, fcr,
):
    rows, tiles, nz, ny = dims
    nyh = ny // YLO
    rb = rows // BS
    chunk = nz * SEND
    blk, grp = lax.axis_index("blk"), lax.axis_index("grp")
    core = grp % 2
    z = (grp // 2) % nz
    y = (grp // (2 * nz)) * YLO + blk % YLO
    x = blk // YLO

    def at(x_, y_, z_, core_):
        return {"blk": x_ * YLO + y_ % YLO, "grp": ((y_ // YLO) * nz + z_) * 2 + core_}

    def wrap(v, n):
        return lax.rem(v + n, n)

    def copy(src, dst, send, recv, to):
        return pltpu.make_async_remote_copy(
            src_ref=src, dst_ref=dst, send_sem=send, recv_sem=recv, device_id=to, device_id_type=MESH
        )

    to_z = {k: at(x, y, wrap(z + k, nz), core) for k in range(1, nz)}
    to_y = {k: at(x, wrap(y + k, ny), z, core) for k in range(1, ny)}
    to_x = {k: at(wrap(x + k, NX), y, z, core) for k in range(1, NX)}
    twin = at(x, y, z, 1 - core)

    loads = [
        pltpu.make_async_copy(feat_hbm, xn.at[:, pl.ds(0, F_IN)], load_sem.at[0]),
        pltpu.make_async_copy(vals_hbm.at[0, 0], vals, load_sem.at[1]),
        pltpu.make_async_copy(gout_hbm, gout, load_sem.at[2]),
        pltpu.make_async_copy(ws_hbm, w.at[pl.ds(0, F_IN)], load_sem.at[3]),
        pltpu.make_async_copy(wn_hbm, w.at[pl.ds(F_IN, F_IN)], load_sem.at[4]),
    ]
    for load in loads:
        load.start()

    barrier = pltpu.get_barrier_semaphore()
    partners = [*to_z.values(), *to_y.values(), *to_x.values(), twin]
    for partner in partners:
        pl.semaphore_signal(barrier, inc=1, device_id=partner, device_id_type=MESH)

    loads[0].wait()
    picked = []
    lanes = lax.broadcasted_iota(jnp.int32, (16, F_IN), 0)
    for j in range(SEND):
        row = send_rows[0, 0, j]
        group = xn[pl.ds((row >> 4) * 16, 16), pl.ds(0, F_IN)].astype(jnp.float32)
        picked.append(jnp.sum(jnp.where(lanes == (row & 15), group, 0.0), axis=0, keepdims=True))
    mine[...] = jnp.concatenate(picked, axis=0)

    pl.semaphore_wait(barrier, len(partners))

    sent = []
    for k in reversed(ring_order(nz)):
        c = copy(mine, zbuf.at[z], zs.at[k], zr.at[k], to_z[k])
        c.start()
        sent.append(c)
    zbuf[z] = mine[...]

    loads[1].wait()
    source = lax.broadcasted_iota(jnp.int32, (BS, BS), 0)
    target = lax.broadcasted_iota(jnp.int32, (BS, BS), 1)
    wanted = ((target % 64) // SEND) * (2 * SEND) + (target // 64) * SEND + target % SEND
    order = (source == wanted).astype(jnp.bfloat16)

    @pl.loop(0, tiles // 4)
    def _(i):
        block = vals[pl.ds(i * 4, 4)].reshape(4 * BS, BS)
        moved = jnp.dot(block, order, preferred_element_type=jnp.float32)
        vals[pl.ds(i * 4, 4)] = moved.astype(jnp.bfloat16).reshape(4, BS, BS)

    def latest(r, end):
        return lax.fori_loop(
            0, end, lambda s, best: jnp.maximum(best, (tile_rows[0, 0, s] == r).astype(jnp.int32) * (s + 1)), jnp.int32(0)
        )

    @pl.loop(0, tiles)
    def _(t):
        links[t] = latest(tile_rows[0, 0, t], t)

    @pl.loop(0, rb)
    def _(r):
        links[64 + r] = latest(r, tiles)

    prods[0] = jnp.zeros((BS, F_IN), jnp.float32)

    def place(x_, y_):
        return pl.ds(pl.multiple_of(((x_ * YLO + y_ % YLO) * nyh + y_ // YLO) * chunk, 32), chunk)

    def slab_of(x_):
        return pl.ds(pl.multiple_of(x_ * (ny * chunk), 32), ny * chunk)

    for k in ring_order(nz):
        copy(mine, zbuf.at[wrap(z - k, nz)], zs.at[k], zr.at[k], to_z[k]).wait_recv()
    shared[core, place(x, y)] = zbuf[...].reshape(chunk, F_IN).astype(jnp.bfloat16)

    def send_x(k):
        where = shared.at[core, place(x, wrap(y - k, ny))]
        for i, step in enumerate((1, NX - 1)):
            c = copy(where, where, xs.at[i, k], xr.at[i, k], to_x[step])
            c.start()
            sent.append(c)

    send_x(0)
    own = shared.at[core, place(x, y)]
    for k in reversed(ring_order(ny)):
        c = copy(own, own, ys.at[k], yr.at[k], to_y[k])
        c.start()
        sent.append(c)
    for k in ring_order(ny):
        where = shared.at[core, place(x, wrap(y - k, ny))]
        copy(where, where, ys.at[k], yr.at[k], to_y[k]).wait_recv()
        send_x(k)

    def to_twin(i, x_):
        where = shared.at[core, slab_of(x_)]
        c = copy(where, where, cs.at[i], cr.at[i], twin)
        c.start()
        sent.append(c)

    to_twin(0, x)
    for k in (0, *ring_order(ny)):
        for i, step in enumerate((1, NX - 1)):
            where = shared.at[core, place(wrap(x - step, NX), wrap(y - k, ny))]
            copy(where, where, xs.at[i, k], xr.at[i, k], to_x[step]).wait_recv()
            if (k < ny // 2) == (i == 0):
                c = copy(where, where, rs.at[k], rr.at[k], to_x[step])
                c.start()
                sent.append(c)
    to_twin(1, wrap(x - 1, NX))
    to_twin(2, wrap(x + 1, NX))
    for k in (0, *ring_order(ny)):
        where = shared.at[core, place(wrap(x + 2, NX), wrap(y - k, ny))]
        copy(where, where, rs.at[k], rr.at[k], to_x[1]).wait_recv()
    to_twin(3, wrap(x + 2, NX))
    for i, x_ in enumerate((x, wrap(x - 1, NX), wrap(x + 1, NX), wrap(x + 2, NX))):
        where = shared.at[1 - core, slab_of(x_)]
        copy(where, where, cs.at[i], cr.at[i], twin).wait_recv()

    for t in range(tiles):
        here = pl.ds(tile_cols[0, 0, t] * 64, 64)
        taken = jnp.concatenate([shared[0, here], shared[1, here]], axis=0)
        prods[t + 1] = jnp.dot(vals[t], taken, preferred_element_type=jnp.float32)

    @pl.loop(0, tiles)
    def _(t):
        prods[t + 1] = prods[t + 1] + prods[links[t]]

    for load in loads[2:]:
        load.wait()
    step_rows = 2 * BS

    @pl.loop(0, rows // step_rows)
    def _(i):
        here = pl.ds(pl.multiple_of(i * step_rows, step_rows), step_rows)
        neigh = jnp.concatenate([prods[links[64 + 2 * i]], prods[links[65 + 2 * i]]], axis=0)
        xn[here, pl.ds(F_IN, F_IN)] = neigh.astype(jnp.bfloat16)
        pre = jnp.dot(xn[here], w[...], preferred_element_type=jnp.float32) + bias_ref[...]
        sig = jax.nn.sigmoid(pre)
        act[here] = (pre * sig).astype(jnp.bfloat16)
        gp[here] = (gout[here].astype(jnp.float32) * sig * (1.0 + pre * (1.0 - sig))).astype(jnp.bfloat16)

    act_out = pltpu.make_async_copy(act, act_hbm, out_sem)
    act_out.start()
    grads = lax.dot_general(xn[...], gp[...], (((0,), (0,)), ((), ())), preferred_element_type=jnp.float32)
    for s in range(2):
        for m in range(32):
            r, l = F_IN * s + 8 * (m // 2), 128 * (m % 2)
            part[s, m] = grads[r:r + 8, l:l + 128]

    c = copy(part.at[1 - core], rx_core, r0, r1, twin)
    c.start()
    sent.append(c)
    c.wait_recv()
    half[...] = part[core] + rx_core[...]
    per = 32 // NX
    for k in (2, 1, 3):
        c = copy(half.at[pl.ds(wrap(x + k, NX) * per, per)], rx_x.at[k], rxs.at[k], rxr.at[k], to_x[k])
        c.start()
        sent.append(c)
    for k in (1, 3, 2):
        copy(half.at[pl.ds(0, per)], rx_x.at[k], rxs.at[k], rxr.at[k], to_x[k]).wait_recv()
    slab[...] = half[pl.ds(x * per, per)] + rx_x[1] + rx_x[2] + rx_x[3]
    each = per // ny
    for k in reversed(ring_order(ny)):
        c = copy(slab.at[pl.ds(wrap(y + k, ny) * each, each)], rx_y.at[k], rys.at[k], ryr.at[k], to_y[k])
        c.start()
        sent.append(c)
    total = slab[pl.ds(y * each, each)]
    for k in ring_order(ny):
        copy(slab.at[pl.ds(0, each)], rx_y.at[k], rys.at[k], ryr.at[k], to_y[k]).wait_recv()
        total = total + rx_y[k]
    tile[...] = total
    for k in reversed(ring_order(nz)):
        c = copy(tile, rx_z.at[z], rzs.at[k], rzr.at[k], to_z[k])
        c.start()
        sent.append(c)
    rx_z[z] = total
    for k in ring_order(nz):
        copy(tile, rx_z.at[wrap(z - k, nz)], rzs.at[k], rzr.at[k], to_z[k]).wait_recv()
    total = rx_z[0]
    for k in range(1, nz):
        total = total + rx_z[k]
    nodes = rows * lax.axis_size("blk") * lax.axis_size("grp")
    factor = 1.0 / jnp.sqrt(jnp.float32(nodes))

    def share(x_, y_):
        return pl.ds(x_ * per + y_ * each, each)

    final[core, share(x, y)] = total * factor
    own = final.at[core, share(x, y)]
    for k in reversed(ring_order(ny)):
        c = copy(own, own, fys.at[k], fyr.at[k], to_y[k])
        c.start()
        sent.append(c)
    for k in ring_order(ny):
        where = final.at[core, share(x, wrap(y - k, ny))]
        copy(where, where, fys.at[k], fyr.at[k], to_y[k]).wait_recv()
    own = final.at[core, pl.ds(x * per, per)]
    for k in (2, 1, 3):
        c = copy(own, own, fxs.at[k], fxr.at[k], to_x[k])
        c.start()
        sent.append(c)
    c = copy(own, own, fcs.at[0], fcr.at[0], twin)
    c.start()
    sent.append(c)
    for k in (1, 3, 2):
        where = final.at[core, pl.ds(wrap(x - k, NX) * per, per)]
        copy(where, where, fxs.at[k], fxr.at[k], to_x[k]).wait_recv()
        c = copy(where, where, fcs.at[k], fcr.at[k], twin)
        c.start()
        sent.append(c)
    for k in range(NX):
        where = final.at[1 - core, pl.ds(wrap(x - k, NX) * per, per)]
        copy(where, where, fcs.at[k], fcr.at[k], twin).wait_recv()
    for s, ref in enumerate((gs_ref, gn_ref)):
        for m in range(32):
            ref[8 * (m // 2):8 * (m // 2) + 8, 128 * (m % 2):128 * (m % 2) + 128] = final[s, m]
    for c in sent:
        c.wait_send()
    act_out.wait()


def shards(mesh_shape, features, send_rows, tile_rows, tile_cols, tile_vals, w_self, w_neigh, bias, grad_out):
    rows = features.shape[0]
    tiles = tile_vals.shape[2]
    nx_ylo, rest = mesh_shape
    nyh = 4
    nz = rest // (2 * nyh)
    ny = nyh * YLO
    ndev = nx_ylo * rest
    per = 32 // NX
    each = per // ny
    bf16, f32 = jnp.bfloat16, jnp.float32
    dma = pltpu.SemaphoreType.DMA
    smem = pl.BlockSpec(memory_space=pltpu.SMEM)
    anywhere = pl.BlockSpec(memory_space=pl.ANY)
    vmem = pl.BlockSpec(memory_space=pltpu.VMEM)
    return pl.pallas_call(
        functools.partial(kernel, (rows, tiles, nz, ny)),
        out_shape=(
            jax.ShapeDtypeStruct((rows, HID), bf16),
            jax.ShapeDtypeStruct((F_IN, HID), f32),
            jax.ShapeDtypeStruct((F_IN, HID), f32),
        ),
        in_specs=[smem, smem, smem, anywhere, anywhere, anywhere, anywhere, vmem, anywhere],
        out_specs=(anywhere, vmem, vmem),
        scratch_shapes=[
            pltpu.VMEM((rows, 2 * F_IN), bf16),
            pltpu.VMEM((2 * F_IN, HID), bf16),
            pltpu.VMEM((tiles, BS, BS), bf16),
            pltpu.VMEM((rows, HID), bf16),
            pltpu.VMEM((rows, HID), bf16),
            pltpu.VMEM((rows, HID), bf16),
            pltpu.VMEM((nz, SEND, F_IN), f32),
            pltpu.VMEM((SEND, F_IN), f32),
            pltpu.VMEM((2, ndev // 2 * SEND, F_IN), bf16),
            pltpu.VMEM((tiles + 1, BS, F_IN), f32),
            pltpu.SMEM((128,), jnp.int32),
            pltpu.VMEM((2, 32, 8, 128), f32),
            pltpu.VMEM((32, 8, 128), f32),
            pltpu.VMEM((32, 8, 128), f32),
            pltpu.VMEM((NX, per, 8, 128), f32),
            pltpu.VMEM((per, 8, 128), f32),
            pltpu.VMEM((ny, each, 8, 128), f32),
            pltpu.VMEM((each, 8, 128), f32),
            pltpu.VMEM((nz, each, 8, 128), f32),
            pltpu.VMEM((2, 32, 8, 128), f32),
            dma((5,)), dma,
            dma((nz,)), dma((nz,)), dma((ny,)), dma((ny,)), dma((2, ny)), dma((2, ny)),
            dma((ny,)), dma((ny,)), dma((4,)), dma((4,)),
            dma, dma, dma((NX,)), dma((NX,)), dma((ny,)), dma((ny,)), dma((nz,)), dma((nz,)),
            dma((ny,)), dma((ny,)), dma((NX,)), dma((NX,)), dma((NX,)), dma((NX,)),
        ],
        compiler_params=pltpu.CompilerParams(
            collective_id=0, has_side_effects=True, vmem_limit_bytes=40 * 1024 * 1024
        ),
    )(send_rows, tile_rows, tile_cols, features, tile_vals, w_self, w_neigh, bias.reshape(1, HID), grad_out)


def solution(mesh):
    in_specs = (
        P(("blk", "grp"), None),
        P("blk", "grp", None),
        P("blk", "grp", None),
        P("blk", "grp", None),
        P("blk", "grp", None, None, None),
        P(),
        P(),
        P(),
        P(("blk", "grp"), None),
    )
    out_specs = (P(("blk", "grp"), None), P(), P())
    body = functools.partial(shards, (mesh.shape["blk"], mesh.shape["grp"]))
    return jax.shard_map(body, mesh=mesh, in_specs=in_specs, out_specs=out_specs, check_vma=False)
```

```python
import functools

import jax
import jax.numpy as jnp
from jax import lax
from jax.experimental import pallas as pl
from jax.experimental.pallas import tpu as pltpu
from jax.sharding import PartitionSpec as P

MESH = pl.DeviceIdType.MESH
BS = 128
F_IN = 128
HID = 256
SEND = 8
NX = 4
YLO = 2


def ring_order(n):
    return sorted(range(1, n), key=lambda k: (min(k, n - k), k))


def kernel(
    dims,
    send_hbm, trows_hbm, tcols_hbm,
    feat_hbm, vals_hbm, ws_hbm, wn_hbm, bias_hbm, gout_hbm,
    act, gs_ref, gn_ref,
    send_rows, tile_rows, tile_cols, bias_ref, xn, w, vals, gout, gp, zbuf, mine, shared, prods, links,
    part, rx_core, half, rx_xy, tile, rx_z, final,
    load_sem,
    zs, zr, ys, yr, xs, xr, rs, rr, cs, cr,
    r0, r1, rxs, rxr, rzs, rzr, fxs, fxr, fcs, fcr,
):
    rows, tiles, nz, ny = dims
    nyh = ny // YLO
    rb = rows // BS
    chunk = nz * SEND
    blk, grp = lax.axis_index("blk"), lax.axis_index("grp")
    core = grp % 2
    z = (grp // 2) % nz
    y = (grp // (2 * nz)) * YLO + blk % YLO
    x = blk // YLO

    def at(x_, y_, z_, core_):
        return {"blk": x_ * YLO + y_ % YLO, "grp": ((y_ // YLO) * nz + z_) * 2 + core_}

    def wrap(v, n):
        return lax.rem(v + n, n)

    def copy(src, dst, send, recv, to):
        return pltpu.make_async_remote_copy(
            src_ref=src, dst_ref=dst, send_sem=send, recv_sem=recv, device_id=to, device_id_type=MESH
        )

    to_z = {k: at(x, y, wrap(z + k, nz), core) for k in range(1, nz)}
    to_y = {k: at(x, wrap(y + k, ny), z, core) for k in range(1, ny)}
    to_x = {k: at(wrap(x + k, NX), y, z, core) for k in (1, NX - 1)}
    twin = at(x, y, z, 1 - core)

    loads = [
        pltpu.make_async_copy(feat_hbm, xn.at[:, pl.ds(0, F_IN)], load_sem.at[0]),
        pltpu.make_async_copy(vals_hbm.at[0, 0], vals, load_sem.at[1]),
        pltpu.make_async_copy(gout_hbm, gout, load_sem.at[2]),
        pltpu.make_async_copy(ws_hbm, w.at[pl.ds(0, F_IN)], load_sem.at[3]),
        pltpu.make_async_copy(wn_hbm, w.at[pl.ds(F_IN, F_IN)], load_sem.at[4]),
        pltpu.make_async_copy(bias_hbm, bias_ref, load_sem.at[5]),
        pltpu.make_async_copy(tcols_hbm, tile_cols, load_sem.at[6]),
        pltpu.make_async_copy(trows_hbm, tile_rows, load_sem.at[7]),
        pltpu.make_async_copy(send_hbm, send_rows, load_sem.at[8]),
    ]
    for load in reversed(loads):
        load.start()

    barrier = pltpu.get_barrier_semaphore()
    partners = [*to_z.values(), *to_y.values(), *to_x.values(), twin]
    for partner in partners:
        pl.semaphore_signal(barrier, inc=1, device_id=partner, device_id_type=MESH)

    loads[8].wait()
    loads[0].wait()
    picked = []
    lanes = lax.broadcasted_iota(jnp.int32, (16, F_IN), 0)
    for j in range(SEND):
        row = send_rows[0, 0, j]
        group = xn[pl.ds((row >> 4) * 16, 16), pl.ds(0, F_IN)].astype(jnp.float32)
        picked.append(jnp.sum(jnp.where(lanes == (row & 15), group, 0.0), axis=0, keepdims=True))
    mine[...] = jnp.concatenate(picked, axis=0)

    pl.semaphore_wait(barrier, len(partners))

    sent = []
    for k in reversed(ring_order(nz)):
        c = copy(mine, zbuf.at[z], zs.at[k], zr.at[k], to_z[k])
        c.start()
        sent.append(c)
    zbuf[z] = mine[...]

    loads[1].wait()
    loads[7].wait()
    source = lax.broadcasted_iota(jnp.int32, (BS, BS), 0)
    target = lax.broadcasted_iota(jnp.int32, (BS, BS), 1)
    wanted = ((target % 64) // SEND) * (2 * SEND) + (target // 64) * SEND + target % SEND
    order = (source == wanted).astype(jnp.bfloat16)

    @pl.loop(0, tiles // 4)
    def _(i):
        block = vals[pl.ds(i * 4, 4)].reshape(4 * BS, BS)
        moved = jnp.dot(block, order, preferred_element_type=jnp.float32)
        vals[pl.ds(i * 4, 4)] = moved.astype(jnp.bfloat16).reshape(4, BS, BS)

    row_of = [tile_rows[0, 0, t] for t in range(tiles)]

    @pl.loop(0, tiles)
    def _(t):
        own = tile_rows[0, 0, t]
        best = jnp.int32(0)
        for s in range(tiles):
            best = jnp.maximum(best, ((row_of[s] == own) & (s < t)).astype(jnp.int32) * (s + 1))
        links[t] = best

    @pl.loop(0, rb)
    def _(r):
        best = jnp.int32(0)
        for s in range(tiles):
            best = jnp.maximum(best, (row_of[s] == r).astype(jnp.int32) * (s + 1))
        links[64 + r] = best

    prods[0] = jnp.zeros((BS, F_IN), jnp.float32)

    def place(x_, y_):
        return pl.ds(pl.multiple_of(((x_ * YLO + y_ % YLO) * nyh + y_ // YLO) * chunk, 32), chunk)

    for k in ring_order(nz):
        copy(mine, zbuf.at[wrap(z - k, nz)], zs.at[k], zr.at[k], to_z[k]).wait_recv()
    shared[core, place(x, y)] = zbuf[...].reshape(chunk, F_IN).astype(jnp.bfloat16)

    def send_x(k):
        where = shared.at[core, place(x, wrap(y - k, ny))]
        for i, step in enumerate((1, NX - 1)):
            c = copy(where, where, xs.at[i, k], xr.at[i, k], to_x[step])
            c.start()
            sent.append(c)

    def to_twin(far, k):
        where = shared.at[core, place(wrap(x - far, NX), wrap(y - k, ny))]
        c = copy(where, where, cs.at[far, k], cr.at[far, k], twin)
        c.start()
        sent.append(c)

    def from_y(k):
        where = shared.at[core, place(x, wrap(y - k, ny))]
        copy(where, where, ys.at[k], yr.at[k], to_y[k]).wait_recv()
        send_x(k)
        to_twin(0, k)

    def from_x(k):
        for i, step in enumerate((1, NX - 1)):
            where = shared.at[core, place(wrap(x - step, NX), wrap(y - k, ny))]
            copy(where, where, xs.at[i, k], xr.at[i, k], to_x[step]).wait_recv()
            if (k < ny // 2) == (i == 0):
                c = copy(where, where, rs.at[k], rr.at[k], to_x[step])
                c.start()
                sent.append(c)
            to_twin(step, k)

    send_x(0)
    own = shared.at[core, place(x, y)]
    for k in reversed(ring_order(ny)):
        c = copy(own, own, ys.at[k], yr.at[k], to_y[k])
        c.start()
        sent.append(c)
    to_twin(0, 0)
    arrivals = ring_order(ny)
    behind = [0, *arrivals]
    for n, k in enumerate(arrivals):
        from_y(k)
        if n != 1:
            from_x(behind.pop(0))
    for k in behind:
        from_x(k)
    for k in (0, *arrivals):
        where = shared.at[core, place(wrap(x + 2, NX), wrap(y - k, ny))]
        copy(where, where, rs.at[k], rr.at[k], to_x[1]).wait_recv()
        to_twin(2, k)
    for far in (0, 1, 3, 2):
        for k in (0, *arrivals):
            where = shared.at[1 - core, place(wrap(x - far, NX), wrap(y - k, ny))]
            copy(where, where, cs.at[far, k], cr.at[far, k], twin).wait_recv()

    loads[6].wait()
    for t in range(tiles):
        here = pl.ds(tile_cols[0, 0, t] * 64, 64)
        taken = jnp.concatenate([shared[0, here], shared[1, here]], axis=0)
        prods[t + 1] = jnp.dot(vals[t], taken, preferred_element_type=jnp.float32)

    @pl.loop(0, tiles)
    def _(t):
        prods[t + 1] = prods[t + 1] + prods[links[t]]

    for load in loads[2:6]:
        load.wait()
    step_rows = 2 * BS

    @pl.loop(0, rows // step_rows)
    def _(i):
        here = pl.ds(pl.multiple_of(i * step_rows, step_rows), step_rows)
        neigh = jnp.concatenate([prods[links[64 + 2 * i]], prods[links[65 + 2 * i]]], axis=0)
        xn[here, pl.ds(F_IN, F_IN)] = neigh.astype(jnp.bfloat16)
        pre = jnp.dot(xn[here], w[...], preferred_element_type=jnp.float32) + bias_ref[...]
        sig = jax.nn.sigmoid(pre)
        act[here] = (pre * sig).astype(jnp.bfloat16)
        gp[here] = (gout[here].astype(jnp.float32) * sig * (1.0 + pre * (1.0 - sig))).astype(jnp.bfloat16)

    grads = lax.dot_general(xn[...], gp[...], (((0,), (0,)), ((), ())), preferred_element_type=jnp.float32)
    for s in range(2):
        for m in range(32):
            r, l = F_IN * s + 8 * (m // 2), 128 * (m % 2)
            part[s, m] = grads[r:r + 8, l:l + 128]

    c = copy(part.at[1 - core], rx_core, r0, r1, twin)
    c.start()
    sent.append(c)
    c.wait_recv()
    half[...] = part[core] + rx_core[...]

    def hops(d):
        return min(d[0], NX - d[0]) + min(d[1], ny - d[1])

    plane = sorted(((i, j) for i in range(NX) for j in range(ny) if i or j), key=hops)

    def to_plane(d):
        return at(wrap(x + d[0], NX), wrap(y + d[1], ny), z, core)

    def tile_of(d, sign):
        return wrap(x + sign * d[0], NX) * ny + wrap(y + sign * d[1], ny)

    for d in reversed(plane):
        c = copy(half.at[tile_of(d, 1)], rx_xy.at[d[0], d[1]], rxs.at[d[0], d[1]], rxr.at[d[0], d[1]], to_plane(d))
        c.start()
        sent.append(c)
    total = half[x * ny + y]
    for d in plane:
        copy(half.at[0], rx_xy.at[d[0], d[1]], rxs.at[d[0], d[1]], rxr.at[d[0], d[1]], to_plane(d)).wait_recv()
        total = total + rx_xy[d[0], d[1]]
    tile[...] = total
    for k in reversed(ring_order(nz)):
        c = copy(tile, rx_z.at[z], rzs.at[k], rzr.at[k], to_z[k])
        c.start()
        sent.append(c)
    rx_z[z] = total
    for k in ring_order(nz):
        copy(tile, rx_z.at[wrap(z - k, nz)], rzs.at[k], rzr.at[k], to_z[k]).wait_recv()
    total = rx_z[0]
    for k in range(1, nz):
        total = total + rx_z[k]
    nodes = rows * lax.axis_size("blk") * lax.axis_size("grp")
    factor = 1.0 / jnp.sqrt(jnp.float32(nodes))
    final[core, x * ny + y] = total * factor
    own = final.at[core, x * ny + y]
    for d in reversed(plane):
        c = copy(own, own, fxs.at[d[0], d[1]], fxr.at[d[0], d[1]], to_plane(d))
        c.start()
        sent.append(c)
    for d in ((0, 0), *plane):
        where = final.at[core, tile_of(d, -1)]
        if d != (0, 0):
            copy(where, where, fxs.at[d[0], d[1]], fxr.at[d[0], d[1]], to_plane(d)).wait_recv()
        c = copy(where, where, fcs.at[d[0], d[1]], fcr.at[d[0], d[1]], twin)
        c.start()
        sent.append(c)
    for d in ((0, 0), *plane):
        where = final.at[1 - core, tile_of(d, -1)]
        copy(where, where, fcs.at[d[0], d[1]], fcr.at[d[0], d[1]], twin).wait_recv()
    for s, ref in enumerate((gs_ref, gn_ref)):
        for m in range(32):
            ref[8 * (m // 2):8 * (m // 2) + 8, 128 * (m % 2):128 * (m % 2) + 128] = final[s, m]
    for c in sent:
        c.wait_send()


def shards(mesh_shape, features, send_rows, tile_rows, tile_cols, tile_vals, w_self, w_neigh, bias, grad_out):
    rows = features.shape[0]
    tiles = tile_vals.shape[2]
    nx_ylo, rest = mesh_shape
    nyh = 4
    nz = rest // (2 * nyh)
    ny = nyh * YLO
    ndev = nx_ylo * rest
    bf16, f32 = jnp.bfloat16, jnp.float32
    dma = pltpu.SemaphoreType.DMA
    hbm = pl.BlockSpec(memory_space=pltpu.HBM)
    vmem = pl.BlockSpec(memory_space=pltpu.VMEM)
    return pl.pallas_call(
        functools.partial(kernel, (rows, tiles, nz, ny)),
        out_shape=(
            jax.ShapeDtypeStruct((rows, HID), bf16),
            jax.ShapeDtypeStruct((F_IN, HID), f32),
            jax.ShapeDtypeStruct((F_IN, HID), f32),
        ),
        in_specs=[hbm] * 9,
        out_specs=(vmem, vmem, vmem),
        scratch_shapes=[
            pltpu.SMEM((1, 1, SEND), jnp.int32),
            pltpu.SMEM((1, 1, tiles), jnp.int32),
            pltpu.SMEM((1, 1, tiles), jnp.int32),
            pltpu.VMEM((1, HID), f32),
            pltpu.VMEM((rows, 2 * F_IN), bf16),
            pltpu.VMEM((2 * F_IN, HID), bf16),
            pltpu.VMEM((tiles, BS, BS), bf16),
            pltpu.VMEM((rows, HID), bf16),
            pltpu.VMEM((rows, HID), bf16),
            pltpu.VMEM((nz, SEND, F_IN), f32),
            pltpu.VMEM((SEND, F_IN), f32),
            pltpu.VMEM((2, ndev // 2 * SEND, F_IN), bf16),
            pltpu.VMEM((tiles + 1, BS, F_IN), f32),
            pltpu.SMEM((128,), jnp.int32),
            pltpu.VMEM((2, 32, 8, 128), f32),
            pltpu.VMEM((32, 8, 128), f32),
            pltpu.VMEM((32, 8, 128), f32),
            pltpu.VMEM((NX, ny, 8, 128), f32),
            pltpu.VMEM((8, 128), f32),
            pltpu.VMEM((nz, 8, 128), f32),
            pltpu.VMEM((2, 32, 8, 128), f32),
            dma((9,)),
            dma((nz,)), dma((nz,)), dma((ny,)), dma((ny,)), dma((2, ny)), dma((2, ny)),
            dma((ny,)), dma((ny,)), dma((NX, ny)), dma((NX, ny)),
            dma, dma, dma((NX, ny)), dma((NX, ny)), dma((nz,)), dma((nz,)),
            dma((NX, ny)), dma((NX, ny)), dma((NX, ny)), dma((NX, ny)),
        ],
        compiler_params=pltpu.CompilerParams(
            collective_id=0, has_side_effects=True, vmem_limit_bytes=40 * 1024 * 1024
        ),
    )(*(
        pltpu.with_memory_space_constraint(a, pltpu.HBM)
        for a in (send_rows, tile_rows, tile_cols, features, tile_vals, w_self, w_neigh, bias.reshape(1, HID), grad_out)
    ))


def solution(mesh):
    in_specs = (
        P(("blk", "grp"), None),
        P("blk", "grp", None),
        P("blk", "grp", None),
        P("blk", "grp", None),
        P("blk", "grp", None, None, None),
        P(),
        P(),
        P(),
        P(("blk", "grp"), None),
    )
    out_specs = (P(("blk", "grp"), None), P(), P())
    body = functools.partial(shards, (mesh.shape["blk"], mesh.shape["grp"]))
    return jax.shard_map(body, mesh=mesh, in_specs=in_specs, out_specs=out_specs, check_vma=False)
```

```python
import functools

import jax
import jax.numpy as jnp
from jax import lax
from jax.experimental import pallas as pl
from jax.experimental.pallas import tpu as pltpu
from jax.sharding import PartitionSpec as P

MESH = pl.DeviceIdType.MESH
BS = 128
F_IN = 128
HID = 256
SEND = 8
NX = 4
YLO = 2


def ring_order(n):
    return sorted(range(1, n), key=lambda k: (min(k, n - k), k))


def kernel(
    dims,
    send_hbm, trows_hbm, tcols_hbm,
    feat_hbm, vals_hbm, ws_hbm, wn_hbm, bias_hbm, gout_hbm,
    act, gs_ref, gn_ref,
    send_rows, tile_rows, tile_cols, bias_ref, xn, w, vals, gout, gp, zbuf, mine, shared, prods, links,
    part, rx_core, half, rx_xy, tile, rx_z, final,
    load_sem, zs, zr, ys, yr, xs, xr, rs, rr, cs, cr, ps, pr, fs, fr,
):
    rows, tiles, nz, ny = dims
    nyh = ny // YLO
    rb = rows // BS
    chunk = nz * SEND
    blk, grp = lax.axis_index("blk"), lax.axis_index("grp")
    core = grp & 1
    yhi = lax.div(grp, 2 * nz)
    z = (grp >> 1) - yhi * nz
    y = yhi * YLO + (blk & 1)
    x = blk >> 1

    xk = [(x + k) & (NX - 1) for k in range(NX)]
    yk = [(y + k) & (ny - 1) for k in range(ny)]
    zk = [z] + [jnp.where(z + k >= nz, z + k - nz, z + k) for k in range(1, nz)]
    y_grp = [(v >> 1) * (2 * nz) for v in yk]
    y_row = [((v & 1) * nyh + (v >> 1)) * chunk for v in yk]
    x_row = [v * (ny * chunk) for v in xk]
    z_core = 2 * z + core

    def on(i, j):
        return {"blk": xk[i] * YLO + (yk[j] & 1), "grp": y_grp[j] + z_core}

    def copy(src, dst, send, recv, to):
        return pltpu.make_async_remote_copy(
            src_ref=src, dst_ref=dst, send_sem=send, recv_sem=recv, device_id=to, device_id_type=MESH
        )

    to_z = {k: {"blk": blk, "grp": y_grp[0] + 2 * zk[k] + core} for k in range(1, nz)}
    to_y = {k: on(0, k) for k in range(1, ny)}
    to_x = {k: on(k, 0) for k in (1, NX - 1)}
    twin = {"blk": blk, "grp": grp + 1 - 2 * core}

    barrier = pltpu.get_barrier_semaphore()
    partners = [*to_z.values(), *to_y.values(), *to_x.values(), twin]
    for partner in partners:
        pl.semaphore_signal(barrier, inc=1, device_id=partner, device_id_type=MESH)

    loads = [
        pltpu.make_async_copy(send_hbm, send_rows, load_sem.at[8]),
        pltpu.make_async_copy(feat_hbm, xn.at[:, pl.ds(0, F_IN)], load_sem.at[0]),
        pltpu.make_async_copy(trows_hbm, tile_rows, load_sem.at[7]),
        pltpu.make_async_copy(vals_hbm.at[0, 0], vals, load_sem.at[1]),
        pltpu.make_async_copy(tcols_hbm, tile_cols, load_sem.at[6]),
        pltpu.make_async_copy(ws_hbm, w.at[pl.ds(0, F_IN)], load_sem.at[3]),
        pltpu.make_async_copy(wn_hbm, w.at[pl.ds(F_IN, F_IN)], load_sem.at[4]),
        pltpu.make_async_copy(bias_hbm, bias_ref, load_sem.at[5]),
        pltpu.make_async_copy(gout_hbm, gout, load_sem.at[2]),
    ]
    for load in loads:
        load.start()
    loads[0].wait()
    loads[1].wait()
    picked = []
    lanes = lax.broadcasted_iota(jnp.int32, (16, F_IN), 0)
    for j in range(SEND):
        row = send_rows[0, 0, j]
        group = xn[pl.ds((row >> 4) * 16, 16), pl.ds(0, F_IN)].astype(jnp.float32)
        picked.append(jnp.sum(jnp.where(lanes == (row & 15), group, 0.0), axis=0, keepdims=True))
    mine[...] = jnp.concatenate(picked, axis=0)

    pl.semaphore_wait(barrier, len(partners))

    for k in reversed(ring_order(nz)):
        copy(mine, zbuf.at[z], zs, zr, to_z[k]).start()
    zbuf[z] = mine[...]

    loads[2].wait()
    loads[3].wait()
    source = lax.broadcasted_iota(jnp.int32, (BS, BS), 0)
    target = lax.broadcasted_iota(jnp.int32, (BS, BS), 1)
    wanted = ((target % 64) // SEND) * (2 * SEND) + (target // 64) * SEND + target % SEND
    order = (source == wanted).astype(jnp.bfloat16)

    @pl.loop(0, tiles // 4)
    def _(i):
        block = vals[pl.ds(i * 4, 4)].reshape(4 * BS, BS)
        moved = jnp.dot(block, order, preferred_element_type=jnp.float32)
        vals[pl.ds(i * 4, 4)] = moved.astype(jnp.bfloat16).reshape(4, BS, BS)

    row_of = [tile_rows[0, 0, t] for t in range(tiles)]

    @pl.loop(0, tiles)
    def _(t):
        own = tile_rows[0, 0, t]
        best = jnp.int32(0)
        for s in range(tiles):
            best = jnp.maximum(best, ((row_of[s] == own) & (s < t)).astype(jnp.int32) * (s + 1))
        links[t] = best

    @pl.loop(0, rb)
    def _(r):
        best = jnp.int32(0)
        for s in range(tiles):
            best = jnp.maximum(best, (row_of[s] == r).astype(jnp.int32) * (s + 1))
        links[64 + r] = best

    prods[0] = jnp.zeros((BS, F_IN), jnp.float32)

    def place(i, j):
        return shared.at[core, pl.ds(pl.multiple_of(x_row[i] + y_row[j], 32), chunk)]

    def slab(core_, i):
        return shared.at[core_, pl.ds(pl.multiple_of(x_row[i], 32), ny * chunk)]

    others = zbuf.at[pl.ds(0, nz - 1)]
    copy(others, others, zs, zr, twin).wait()
    own = place(0, 0)
    own[...] = zbuf[...].reshape(chunk, F_IN).astype(jnp.bfloat16)

    ends = ((1, NX - 1), (NX - 1, 1))

    def send_x(k):
        where = place(0, -k)
        for i, (step, _) in enumerate(ends):
            copy(where, where, xs, xr.at[i, k], to_x[step]).start()

    def from_y(k):
        where = place(0, -k)
        copy(where, where, ys, yr.at[k], to_y[k]).wait_recv()
        send_x(k)

    def from_x(k):
        for i, (step, origin) in enumerate(ends):
            where = place(origin, -k)
            copy(where, where, xs, xr.at[i, k], to_x[step]).wait_recv()
            if (k < ny // 2) == (i == 0):
                copy(where, where, rs, rr, to_x[step]).start()

    def to_twin(i):
        where = slab(core, i)
        copy(where, where, cs, cr.at[i], twin).start()

    send_x(0)
    for k in reversed(ring_order(ny)):
        copy(own, own, ys, yr.at[k], to_y[k]).start()
    arrivals = ring_order(ny)
    behind = [0, *arrivals]
    for n, k in enumerate(arrivals):
        from_y(k)
        if n != 1:
            from_x(behind.pop(0))
    to_twin(0)
    for k in behind:
        from_x(k)
    to_twin(1)
    to_twin(NX - 1)
    where = slab(core, 2)
    copy(where, where, rs, rr, twin).wait_recv()
    to_twin(2)
    loads[4].wait()
    for load in loads[5:]:
        load.wait()
    seven = shared.at[0, pl.ds(0, (ny - 1) * chunk)]
    copy(seven, seven, ys, yr.at[1], twin).wait_send()
    for _ in range(2):
        copy(where, where, xs, xr.at[0, 0], twin).wait_send()
    copy(where, where, rs, rr, twin).wait_send()
    for i in (0, 1, NX - 1, 2):
        where = slab(1 - core, i)
        copy(where, where, cs, cr.at[i], twin).wait()

    for t in range(tiles):
        here = pl.ds(tile_cols[0, 0, t] * 64, 64)
        taken = jnp.concatenate([shared[0, here], shared[1, here]], axis=0)
        prods[t + 1] = jnp.dot(vals[t], taken, preferred_element_type=jnp.float32)

    @pl.loop(0, tiles)
    def _(t):
        prods[t + 1] = prods[t + 1] + prods[links[t]]

    step_rows = 2 * BS

    @pl.loop(0, rows // step_rows)
    def _(i):
        here = pl.ds(pl.multiple_of(i * step_rows, step_rows), step_rows)
        neigh = jnp.concatenate([prods[links[64 + 2 * i]], prods[links[65 + 2 * i]]], axis=0)
        xn[here, pl.ds(F_IN, F_IN)] = neigh.astype(jnp.bfloat16)
        pre = jnp.dot(xn[here], w[...], preferred_element_type=jnp.float32) + bias_ref[...]
        sig = jax.nn.sigmoid(pre)
        act[here] = (pre * sig).astype(jnp.bfloat16)
        gp[here] = (gout[here].astype(jnp.float32) * sig * (1.0 + pre * (1.0 - sig))).astype(jnp.bfloat16)

    grads = lax.dot_general(xn[...], gp[...], (((0,), (0,)), ((), ())), preferred_element_type=jnp.float32)
    for s in range(2):
        for m in range(32):
            r, l = F_IN * s + 8 * (m // 2), 128 * (m % 2)
            part[s, m] = grads[r:r + 8, l:l + 128]

    c = copy(part.at[1 - core], rx_core, ps.at[0], pr.at[0], twin)
    c.start()
    c.wait_recv()
    half[...] = part[core] + rx_core[...]
    plane = [(i, j) for i in range(NX) for j in range(ny) if i or j]
    plane.sort(key=lambda d: -min(d[0], NX - d[0]) - min(d[1], ny - d[1]))
    x_tile = [v * ny for v in xk]
    for i, j in plane:
        copy(half.at[x_tile[i] + yk[j]], rx_xy.at[i * ny + j - 1], ps.at[1], pr.at[1], on(i, j)).start()
    c.wait_send()
    count = NX * ny - 1
    most = rx_xy.at[pl.ds(0, count)]
    copy(most, most, ps.at[1], pr.at[1], twin).wait()
    total = half[x_tile[0] + y]
    for n in range(count):
        total = total + rx_xy[n]
    tile[...] = total
    for k in reversed(ring_order(nz)):
        copy(tile, rx_z.at[z], ps.at[2], pr.at[2], to_z[k]).start()
    rx_z[z] = total
    others = rx_z.at[pl.ds(0, nz - 1)]
    copy(others, others, ps.at[2], pr.at[2], twin).wait()
    total = rx_z[0]
    for k in range(1, nz):
        total = total + rx_z[k]
    nodes = rows * lax.axis_size("blk") * lax.axis_size("grp")
    factor = 1.0 / jnp.sqrt(jnp.float32(nodes))
    own = final.at[core, x_tile[0] + y]
    own[...] = total * factor
    for i, j in plane:
        copy(own, own, fs.at[0], fr.at[0], on(i, j)).start()
    most = final.at[0, pl.ds(0, count)]
    copy(most, most, fs.at[0], fr.at[0], twin).wait()
    c = copy(final.at[core], final.at[core], fs.at[1], fr.at[1], twin)
    c.start()
    c.wait_send()
    copy(final.at[1 - core], final.at[1 - core], fs.at[1], fr.at[1], twin).wait_recv()
    for s, ref in enumerate((gs_ref, gn_ref)):
        for m in range(32):
            ref[8 * (m // 2):8 * (m // 2) + 8, 128 * (m % 2):128 * (m % 2) + 128] = final[s, m]


def store(act, gs, gn, act_out, gs_out, gn_out, sem):
    copies = [
        pltpu.make_async_copy(src, dst, sem.at[i])
        for i, (src, dst) in enumerate(((act, act_out), (gs, gs_out), (gn, gn_out)))
    ]
    for c in copies:
        c.start()
    for c in copies:
        c.wait()


def shards(mesh_shape, features, send_rows, tile_rows, tile_cols, tile_vals, w_self, w_neigh, bias, grad_out):
    rows = features.shape[0]
    tiles = tile_vals.shape[2]
    nx_ylo, rest = mesh_shape
    nyh = 4
    nz = rest // (2 * nyh)
    ny = nyh * YLO
    ndev = nx_ylo * rest
    bf16, f32 = jnp.bfloat16, jnp.float32
    dma = pltpu.SemaphoreType.DMA
    hbm = pl.BlockSpec(memory_space=pltpu.HBM)
    vmem = pl.BlockSpec(memory_space=pltpu.VMEM)
    outs = (
        jax.ShapeDtypeStruct((rows, HID), bf16),
        jax.ShapeDtypeStruct((F_IN, HID), f32),
        jax.ShapeDtypeStruct((F_IN, HID), f32),
    )
    results = pl.pallas_call(
        functools.partial(kernel, (rows, tiles, nz, ny)),
        out_shape=outs,
        in_specs=[hbm] * 9,
        out_specs=(vmem, vmem, vmem),
        scratch_shapes=[
            pltpu.SMEM((1, 1, SEND), jnp.int32),
            pltpu.SMEM((1, 1, tiles), jnp.int32),
            pltpu.SMEM((1, 1, tiles), jnp.int32),
            pltpu.VMEM((1, HID), f32),
            pltpu.VMEM((rows, 2 * F_IN), bf16),
            pltpu.VMEM((2 * F_IN, HID), bf16),
            pltpu.VMEM((tiles, BS, BS), bf16),
            pltpu.VMEM((rows, HID), bf16),
            pltpu.VMEM((rows, HID), bf16),
            pltpu.VMEM((nz, SEND, F_IN), f32),
            pltpu.VMEM((SEND, F_IN), f32),
            pltpu.VMEM((2, ndev // 2 * SEND, F_IN), bf16),
            pltpu.VMEM((tiles + 1, BS, F_IN), f32),
            pltpu.SMEM((128,), jnp.int32),
            pltpu.VMEM((2, 32, 8, 128), f32),
            pltpu.VMEM((32, 8, 128), f32),
            pltpu.VMEM((32, 8, 128), f32),
            pltpu.VMEM((NX * ny, 8, 128), f32),
            pltpu.VMEM((8, 128), f32),
            pltpu.VMEM((nz, 8, 128), f32),
            pltpu.VMEM((2, 32, 8, 128), f32),
            dma((9,)), dma, dma, dma, dma((ny,)), dma, dma((2, ny)), dma, dma, dma, dma((NX,)),
            dma((3,)), dma((3,)), dma((2,)), dma((2,)),
        ],
        compiler_params=pltpu.CompilerParams(
            collective_id=0, has_side_effects=True, vmem_limit_bytes=40 * 1024 * 1024
        ),
    )(*(
        pltpu.with_memory_space_constraint(a, pltpu.HBM)
        for a in (send_rows, tile_rows, tile_cols, features, tile_vals, w_self, w_neigh, bias.reshape(1, HID), grad_out)
    ))
    anywhere = pl.BlockSpec(memory_space=pl.ANY)
    return pl.pallas_call(
        store,
        out_shape=outs,
        in_specs=[anywhere] * 3,
        out_specs=(anywhere,) * 3,
        scratch_shapes=[dma((3,))],
    )(*results)


def solution(mesh):
    in_specs = (
        P(("blk", "grp"), None),
        P("blk", "grp", None),
        P("blk", "grp", None),
        P("blk", "grp", None),
        P("blk", "grp", None, None, None),
        P(),
        P(),
        P(),
        P(("blk", "grp"), None),
    )
    out_specs = (P(("blk", "grp"), None), P(), P())
    body = functools.partial(shards, (mesh.shape["blk"], mesh.shape["grp"]))
    return jax.shard_map(body, mesh=mesh, in_specs=in_specs, out_specs=out_specs, check_vma=False)
```

```python
import functools

import jax
import jax.numpy as jnp
from jax import lax
from jax.experimental import pallas as pl
from jax.experimental.pallas import tpu as pltpu
from jax.sharding import PartitionSpec as P

MESH = pl.DeviceIdType.MESH
BS = 128
F_IN = 128
HID = 256
SEND = 8
NX = 4
YLO = 2


def ring_order(n):
    return sorted(range(1, n), key=lambda k: (min(k, n - k), k))


def kernel(
    dims,
    send_hbm, trows_hbm, tcols_hbm,
    feat_hbm, vals_hbm, ws_hbm, wn_hbm, bias_hbm, gout_hbm,
    act, gs_ref, gn_ref,
    send_rows, tile_rows, tile_cols, bias_ref, xn, w, vals, gout, gp, zbuf, mine, shared, prods, links,
    part, rx_core, half, rx_xy, tile, rx_z, final,
    load_sem, zs, zr, ys, yr, xs, xr, vs, vr, cs, cr, ps, pr, fs, fr,
):
    rows, tiles, nz, ny = dims
    nyh = ny // YLO
    rb = rows // BS
    chunk = nz * SEND
    blk, grp = lax.axis_index("blk"), lax.axis_index("grp")
    core = grp & 1
    yhi = lax.div(grp, 2 * nz)
    z = (grp >> 1) - yhi * nz
    y = yhi * YLO + (blk & 1)
    x = blk >> 1

    xk = [(x + k) & (NX - 1) for k in range(NX)]
    yk = [(y + k) & (ny - 1) for k in range(ny)]
    zk = [z] + [jnp.where(z + k >= nz, z + k - nz, z + k) for k in range(1, nz)]
    y_grp = [(v >> 1) * (2 * nz) for v in yk]
    y_row = [((v & 1) * nyh + (v >> 1)) * chunk for v in yk]
    x_row = [v * (ny * chunk) for v in xk]
    z_core = 2 * z + core

    def on(i, j):
        return {"blk": xk[i] * YLO + (yk[j] & 1), "grp": y_grp[j] + z_core}

    def copy(src, dst, send, recv, to):
        return pltpu.make_async_remote_copy(
            src_ref=src, dst_ref=dst, send_sem=send, recv_sem=recv, device_id=to, device_id_type=MESH
        )

    to_z = {k: {"blk": blk, "grp": y_grp[0] + 2 * zk[k] + core} for k in range(1, nz)}
    to_y = {k: on(0, k) for k in range(1, ny)}
    to_x = {k: on(k, 0) for k in range(1, NX)}
    twin = {"blk": blk, "grp": grp + 1 - 2 * core}

    barrier = pltpu.get_barrier_semaphore()
    partners = [*to_z.values(), *to_y.values(), *to_x.values(), twin]
    for partner in partners:
        pl.semaphore_signal(barrier, inc=1, device_id=partner, device_id_type=MESH)

    loads = [
        pltpu.make_async_copy(send_hbm, send_rows, load_sem.at[8]),
        pltpu.make_async_copy(feat_hbm, xn.at[:, pl.ds(0, F_IN)], load_sem.at[0]),
        pltpu.make_async_copy(trows_hbm, tile_rows, load_sem.at[7]),
        pltpu.make_async_copy(vals_hbm.at[0, 0], vals, load_sem.at[1]),
        pltpu.make_async_copy(tcols_hbm, tile_cols, load_sem.at[6]),
        pltpu.make_async_copy(ws_hbm, w.at[pl.ds(0, F_IN)], load_sem.at[3]),
        pltpu.make_async_copy(wn_hbm, w.at[pl.ds(F_IN, F_IN)], load_sem.at[4]),
        pltpu.make_async_copy(bias_hbm, bias_ref, load_sem.at[5]),
        pltpu.make_async_copy(gout_hbm, gout, load_sem.at[2]),
    ]
    for load in loads:
        load.start()
    loads[0].wait()
    loads[1].wait()
    picked = []
    lanes = lax.broadcasted_iota(jnp.int32, (16, F_IN), 0)
    for j in range(SEND):
        row = send_rows[0, 0, j]
        group = xn[pl.ds((row >> 4) * 16, 16), pl.ds(0, F_IN)].astype(jnp.float32)
        picked.append(jnp.sum(jnp.where(lanes == (row & 15), group, 0.0), axis=0, keepdims=True))
    mine[...] = jnp.concatenate(picked, axis=0)

    pl.semaphore_wait(barrier, len(partners))

    for k in reversed(ring_order(nz)):
        copy(mine, zbuf.at[z], zs, zr, to_z[k]).start()
    zbuf[z] = mine[...]

    loads[2].wait()
    loads[3].wait()
    source = lax.broadcasted_iota(jnp.int32, (BS, BS), 0)
    target = lax.broadcasted_iota(jnp.int32, (BS, BS), 1)
    wanted = ((target % 64) // SEND) * (2 * SEND) + (target // 64) * SEND + target % SEND
    order = (source == wanted).astype(jnp.bfloat16)

    @pl.loop(0, tiles // 4)
    def _(i):
        block = vals[pl.ds(i * 4, 4)].reshape(4 * BS, BS)
        moved = jnp.dot(block, order, preferred_element_type=jnp.float32)
        vals[pl.ds(i * 4, 4)] = moved.astype(jnp.bfloat16).reshape(4, BS, BS)

    row_of = [tile_rows[0, 0, t] for t in range(tiles)]

    @pl.loop(0, tiles)
    def _(t):
        own = tile_rows[0, 0, t]
        best = jnp.int32(0)
        for s in range(tiles):
            best = jnp.maximum(best, ((row_of[s] == own) & (s < t)).astype(jnp.int32) * (s + 1))
        links[t] = best

    @pl.loop(0, rb)
    def _(r):
        best = jnp.int32(0)
        for s in range(tiles):
            best = jnp.maximum(best, (row_of[s] == r).astype(jnp.int32) * (s + 1))
        links[64 + r] = best

    prods[0] = jnp.zeros((BS, F_IN), jnp.float32)

    def place(i, j):
        return shared.at[core, pl.ds(pl.multiple_of(x_row[i] + y_row[j], 32), chunk)]

    def slab(core_, i):
        return shared.at[core_, pl.ds(pl.multiple_of(x_row[i], 32), ny * chunk)]

    others = zbuf.at[pl.ds(0, nz - 1)]
    copy(others, others, zs, zr, twin).wait()
    own = place(0, 0)
    own[...] = zbuf[...].reshape(chunk, F_IN).astype(jnp.bfloat16)

    far_y, near_y, all_x = (2, ny - 2, 4, 3, ny - 3), (1, ny - 1), (2, 1, NX - 1)

    def send(where, sems, to):
        copy(where, where, *sems, to).start()

    def arrived(where, recv):
        copy(where, where, cs, recv, twin).wait_recv()

    for i in all_x:
        send(own, (xs, xr.at[i, 0]), to_x[i])
    for k in (*far_y, *near_y):
        send(own, (ys, yr.at[k]), to_y[k])
    for i in reversed(all_x):
        where = place(-i, 0)
        arrived(where, xr.at[i, 0])
        for n, k in enumerate(near_y):
            send(where, (vs, vr.at[n, i]), to_y[k])
        send(where, (cs, cr.at[i]), twin)
    for k in far_y:
        where = place(0, -k)
        arrived(where, yr.at[k])
        for i in all_x:
            send(where, (xs, xr.at[i, k]), to_x[i])
    for k in near_y:
        arrived(place(0, -k), yr.at[k])
    send(slab(core, 0), (cs, cr.at[0]), twin)

    def from_x(k):
        for i in reversed(all_x):
            where = place(-i, -k)
            arrived(where, xr.at[i, k])
            send(where, (cs, cr.at[i]), twin)

    for k in far_y[:2]:
        from_x(k)
    for i in reversed(all_x):
        for n, k in enumerate(near_y):
            where = place(-i, -k)
            arrived(where, vr.at[n, i])
            send(where, (cs, cr.at[i]), twin)
    for k in far_y[2:]:
        from_x(k)
    loads[4].wait()
    for load in loads[5:]:
        load.wait()

    def all_sent(sem, chunks):
        where = shared.at[0, pl.ds(0, chunks * chunk)]
        copy(where, where, sem, cr.at[0], twin).wait_send()

    all_sent(ys, ny - 1)
    all_sent(xs, 3 * 6)
    all_sent(vs, 3 * 2)
    all_sent(cs, 4 * ny)
    for i in range(NX):
        arrived(slab(1 - core, -i), cr.at[i])

    for t in range(tiles):
        here = pl.ds(tile_cols[0, 0, t] * 64, 64)
        taken = jnp.concatenate([shared[0, here], shared[1, here]], axis=0)
        prods[t + 1] = jnp.dot(vals[t], taken, preferred_element_type=jnp.float32)

    @pl.loop(0, tiles)
    def _(t):
        prods[t + 1] = prods[t + 1] + prods[links[t]]

    step_rows = 2 * BS

    @pl.loop(0, rows // step_rows)
    def _(i):
        here = pl.ds(pl.multiple_of(i * step_rows, step_rows), step_rows)
        neigh = jnp.concatenate([prods[links[64 + 2 * i]], prods[links[65 + 2 * i]]], axis=0)
        xn[here, pl.ds(F_IN, F_IN)] = neigh.astype(jnp.bfloat16)
        pre = jnp.dot(xn[here], w[...], preferred_element_type=jnp.float32) + bias_ref[...]
        sig = jax.nn.sigmoid(pre)
        act[here] = (pre * sig).astype(jnp.bfloat16)
        gp[here] = (gout[here].astype(jnp.float32) * sig * (1.0 + pre * (1.0 - sig))).astype(jnp.bfloat16)

    grads = lax.dot_general(xn[...], gp[...], (((0,), (0,)), ((), ())), preferred_element_type=jnp.float32)
    for s in range(2):
        for m in range(32):
            r, l = F_IN * s + 8 * (m // 2), 128 * (m % 2)
            part[s, m] = grads[r:r + 8, l:l + 128]

    c = copy(part.at[1 - core], rx_core, ps.at[0], pr.at[0], twin)
    c.start()
    c.wait_recv()
    half[...] = part[core] + rx_core[...]
    plane = [(i, j) for i in range(NX) for j in range(ny) if i or j]
    plane.sort(key=lambda d: -min(d[0], NX - d[0]) - min(d[1], ny - d[1]))
    x_tile = [v * ny for v in xk]
    for i, j in plane:
        copy(half.at[x_tile[i] + yk[j]], rx_xy.at[i * ny + j - 1], ps.at[1], pr.at[1], on(i, j)).start()
    c.wait_send()
    count = NX * ny - 1
    most = rx_xy.at[pl.ds(0, count)]
    copy(most, most, ps.at[1], pr.at[1], twin).wait()
    total = half[x_tile[0] + y]
    for n in range(count):
        total = total + rx_xy[n]
    tile[...] = total
    for k in reversed(ring_order(nz)):
        copy(tile, rx_z.at[z], ps.at[2], pr.at[2], to_z[k]).start()
    rx_z[z] = total
    others = rx_z.at[pl.ds(0, nz - 1)]
    copy(others, others, ps.at[2], pr.at[2], twin).wait()
    total = rx_z[0]
    for k in range(1, nz):
        total = total + rx_z[k]
    nodes = rows * lax.axis_size("blk") * lax.axis_size("grp")
    factor = 1.0 / jnp.sqrt(jnp.float32(nodes))
    own = final.at[core, x_tile[0] + y]
    own[...] = total * factor
    for i, j in plane:
        copy(own, own, fs.at[0], fr.at[0], on(i, j)).start()
    most = final.at[0, pl.ds(0, count)]
    copy(most, most, fs.at[0], fr.at[0], twin).wait()
    c = copy(final.at[core], final.at[core], fs.at[1], fr.at[1], twin)
    c.start()
    c.wait_send()
    copy(final.at[1 - core], final.at[1 - core], fs.at[1], fr.at[1], twin).wait_recv()
    for s, ref in enumerate((gs_ref, gn_ref)):
        for m in range(32):
            ref[8 * (m // 2):8 * (m // 2) + 8, 128 * (m % 2):128 * (m % 2) + 128] = final[s, m]


def shards(mesh_shape, features, send_rows, tile_rows, tile_cols, tile_vals, w_self, w_neigh, bias, grad_out):
    rows = features.shape[0]
    tiles = tile_vals.shape[2]
    nx_ylo, rest = mesh_shape
    nyh = 4
    nz = rest // (2 * nyh)
    ny = nyh * YLO
    ndev = nx_ylo * rest
    bf16, f32 = jnp.bfloat16, jnp.float32
    dma = pltpu.SemaphoreType.DMA
    hbm = pl.BlockSpec(memory_space=pltpu.HBM)
    vmem = pl.BlockSpec(memory_space=pltpu.VMEM)
    outs = (
        jax.ShapeDtypeStruct((rows, HID), bf16),
        jax.ShapeDtypeStruct((F_IN, HID), f32),
        jax.ShapeDtypeStruct((F_IN, HID), f32),
    )
    return pl.pallas_call(
        functools.partial(kernel, (rows, tiles, nz, ny)),
        out_shape=outs,
        in_specs=[hbm] * 9,
        out_specs=(vmem, vmem, vmem),
        scratch_shapes=[
            pltpu.SMEM((1, 1, SEND), jnp.int32),
            pltpu.SMEM((1, 1, tiles), jnp.int32),
            pltpu.SMEM((1, 1, tiles), jnp.int32),
            pltpu.VMEM((1, HID), f32),
            pltpu.VMEM((rows, 2 * F_IN), bf16),
            pltpu.VMEM((2 * F_IN, HID), bf16),
            pltpu.VMEM((tiles, BS, BS), bf16),
            pltpu.VMEM((rows, HID), bf16),
            pltpu.VMEM((rows, HID), bf16),
            pltpu.VMEM((nz, SEND, F_IN), f32),
            pltpu.VMEM((SEND, F_IN), f32),
            pltpu.VMEM((2, ndev // 2 * SEND, F_IN), bf16),
            pltpu.VMEM((tiles + 1, BS, F_IN), f32),
            pltpu.SMEM((128,), jnp.int32),
            pltpu.VMEM((2, 32, 8, 128), f32),
            pltpu.VMEM((32, 8, 128), f32),
            pltpu.VMEM((32, 8, 128), f32),
            pltpu.VMEM((NX * ny, 8, 128), f32),
            pltpu.VMEM((8, 128), f32),
            pltpu.VMEM((nz, 8, 128), f32),
            pltpu.VMEM((2, 32, 8, 128), f32),
            dma((9,)), dma, dma, dma, dma((ny,)), dma, dma((NX, ny)), dma, dma((2, NX)), dma, dma((NX,)),
            dma((3,)), dma((3,)), dma((2,)), dma((2,)),
        ],
        compiler_params=pltpu.CompilerParams(
            collective_id=0, has_side_effects=True, vmem_limit_bytes=40 * 1024 * 1024
        ),
    )(*(
        pltpu.with_memory_space_constraint(a, pltpu.HBM)
        for a in (send_rows, tile_rows, tile_cols, features, tile_vals, w_self, w_neigh, bias.reshape(1, HID), grad_out)
    ))


def solution(mesh):
    in_specs = (
        P(("blk", "grp"), None),
        P("blk", "grp", None),
        P("blk", "grp", None),
        P("blk", "grp", None),
        P("blk", "grp", None, None, None),
        P(),
        P(),
        P(),
        P(("blk", "grp"), None),
    )
    out_specs = (P(("blk", "grp"), None), P(), P())
    body = functools.partial(shards, (mesh.shape["blk"], mesh.shape["grp"]))
    return jax.shard_map(body, mesh=mesh, in_specs=in_specs, out_specs=out_specs, check_vma=False)
```

```python
import functools

import jax
import jax.numpy as jnp
from jax import lax
from jax.experimental import pallas as pl
from jax.experimental.pallas import tpu as pltpu
from jax.sharding import PartitionSpec as P

MESH = pl.DeviceIdType.MESH
BS = 128
F_IN = 128
HID = 256
SEND = 8
NX = 4
YLO = 2


def ring_order(n):
    return sorted(range(1, n), key=lambda k: (min(k, n - k), k))


def kernel(
    dims,
    send_hbm, trows_hbm, tcols_hbm,
    feat_hbm, vals_hbm, ws_hbm, wn_hbm, bias_hbm, gout_hbm,
    act, gs_ref, gn_ref,
    send_rows, tile_rows, tile_cols, bias_ref, xn, w, vals, gout, zbuf, mine, shared, prods, links,
    part, rx_core, half, rx_xy, tile, rx_z, final,
    load_sem, zs, zr, ys, yr, xs, xr, vs, vr, cs, cr, ps, pr, fs, fr,
):
    rows, tiles, nz, ny = dims
    nyh = ny // YLO
    rb = rows // BS
    chunk = nz * SEND
    blk, grp = lax.axis_index("blk"), lax.axis_index("grp")
    core = grp & 1
    yhi = lax.div(grp, 2 * nz)
    z = (grp >> 1) - yhi * nz
    y = yhi * YLO + (blk & 1)
    x = blk >> 1

    xk = [(x + k) & (NX - 1) for k in range(NX)]
    yk = [(y + k) & (ny - 1) for k in range(ny)]
    zk = [z] + [jnp.where(z + k >= nz, z + k - nz, z + k) for k in range(1, nz)]
    y_grp = [(v >> 1) * (2 * nz) for v in yk]
    y_row = [((v & 1) * nyh + (v >> 1)) * chunk for v in yk]
    x_row = [v * (ny * chunk) for v in xk]
    z_core = 2 * z + core

    def on(i, j):
        return {"blk": xk[i] * YLO + (yk[j] & 1), "grp": y_grp[j] + z_core}

    def copy(src, dst, send, recv, to):
        return pltpu.make_async_remote_copy(
            src_ref=src, dst_ref=dst, send_sem=send, recv_sem=recv, device_id=to, device_id_type=MESH
        )

    to_z = {k: {"blk": blk, "grp": y_grp[0] + 2 * zk[k] + core} for k in range(1, nz)}
    to_y = {k: on(0, k) for k in range(1, ny)}
    to_x = {k: on(k, 0) for k in range(1, NX)}
    twin = {"blk": blk, "grp": grp + 1 - 2 * core}

    barrier = pltpu.get_barrier_semaphore()
    partners = [*(to_z[k] for k in reversed(ring_order(nz))), *to_y.values(), *to_x.values(), twin]
    for partner in partners:
        pl.semaphore_signal(barrier, inc=1, device_id=partner, device_id_type=MESH)

    loads = [
        pltpu.make_async_copy(send_hbm, send_rows, load_sem.at[8]),
        pltpu.make_async_copy(feat_hbm, xn.at[:, pl.ds(0, F_IN)], load_sem.at[0]),
        pltpu.make_async_copy(trows_hbm, tile_rows, load_sem.at[7]),
        pltpu.make_async_copy(vals_hbm.at[0, 0], vals, load_sem.at[1]),
        pltpu.make_async_copy(tcols_hbm, tile_cols, load_sem.at[6]),
        pltpu.make_async_copy(ws_hbm, w.at[pl.ds(0, F_IN)], load_sem.at[3]),
        pltpu.make_async_copy(wn_hbm, w.at[pl.ds(F_IN, F_IN)], load_sem.at[4]),
        pltpu.make_async_copy(bias_hbm, bias_ref, load_sem.at[5]),
        pltpu.make_async_copy(gout_hbm, gout, load_sem.at[2]),
    ]
    for load in loads:
        load.start()
    loads[0].wait()
    loads[1].wait()
    picked = []
    lanes = lax.broadcasted_iota(jnp.int32, (16, F_IN), 0)
    for j in range(SEND):
        row = send_rows[0, 0, j]
        group = xn[pl.ds((row >> 4) * 16, 16), pl.ds(0, F_IN)].astype(jnp.float32)
        picked.append(jnp.sum(jnp.where(lanes == (row & 15), group, 0.0), axis=0, keepdims=True))
    mine[...] = jnp.concatenate(picked, axis=0)

    pl.semaphore_wait(barrier, len(partners))

    for k in reversed(ring_order(nz)):
        copy(mine, zbuf.at[z], zs, zr, to_z[k]).start()
    zbuf[z] = mine[...]

    loads[2].wait()
    loads[3].wait()
    source = lax.broadcasted_iota(jnp.int32, (BS, BS), 0)
    target = lax.broadcasted_iota(jnp.int32, (BS, BS), 1)
    wanted = ((target % 64) // SEND) * (2 * SEND) + (target // 64) * SEND + target % SEND
    order = (source == wanted).astype(jnp.bfloat16)

    @pl.loop(0, tiles // 4)
    def _(i):
        block = vals[pl.ds(i * 4, 4)].reshape(4 * BS, BS)
        moved = jnp.dot(block, order, preferred_element_type=jnp.float32)
        vals[pl.ds(i * 4, 4)] = moved.astype(jnp.bfloat16).reshape(4, BS, BS)

    row_of = [tile_rows[0, 0, t] for t in range(tiles)]

    @pl.loop(0, tiles)
    def _(t):
        own = tile_rows[0, 0, t]
        best = jnp.int32(0)
        for s in range(tiles):
            best = jnp.maximum(best, ((row_of[s] == own) & (s < t)).astype(jnp.int32) * (s + 1))
        links[t] = best

    @pl.loop(0, rb)
    def _(r):
        best = jnp.int32(0)
        for s in range(tiles):
            best = jnp.maximum(best, (row_of[s] == r).astype(jnp.int32) * (s + 1))
        links[64 + r] = best

    prods[0] = jnp.zeros((BS, F_IN), jnp.float32)

    def place(i, j):
        return shared.at[core, pl.ds(pl.multiple_of(x_row[i] + y_row[j], 32), chunk)]

    def slab(core_, i):
        return shared.at[core_, pl.ds(pl.multiple_of(x_row[i], 32), ny * chunk)]

    others = zbuf.at[pl.ds(0, nz - 1)]
    copy(others, others, zs, zr, twin).wait()
    own = place(0, 0)
    own[...] = zbuf[...].reshape(chunk, F_IN).astype(jnp.bfloat16)

    far_y, near_y, all_x = (2, ny - 2, 4, 3, ny - 3), (1, ny - 1), (2, 1, NX - 1)

    def send(where, sems, to):
        copy(where, where, *sems, to).start()

    def arrived(where, recv):
        copy(where, where, cs, recv, twin).wait_recv()

    for i in all_x:
        send(own, (xs, xr.at[i, 0]), to_x[i])
    for k in (*far_y, *near_y):
        send(own, (ys, yr.at[k]), to_y[k])
    for i in reversed(all_x):
        where = place(-i, 0)
        arrived(where, xr.at[i, 0])
        for n, k in enumerate(near_y):
            send(where, (vs, vr.at[n, i]), to_y[k])
        send(where, (cs, cr.at[i]), twin)
    for k in far_y:
        where = place(0, -k)
        arrived(where, yr.at[k])
        for i in all_x:
            send(where, (xs, xr.at[i, k]), to_x[i])
    for k in near_y:
        arrived(place(0, -k), yr.at[k])
    send(slab(core, 0), (cs, cr.at[0]), twin)

    def from_x(k):
        for i in reversed(all_x):
            where = place(-i, -k)
            arrived(where, xr.at[i, k])
            send(where, (cs, cr.at[i]), twin)

    for k in far_y[:2]:
        from_x(k)
    for i in reversed(all_x):
        for n, k in enumerate(near_y):
            where = place(-i, -k)
            arrived(where, vr.at[n, i])
            send(where, (cs, cr.at[i]), twin)
    for k in far_y[2:]:
        from_x(k)
    loads[4].wait()
    for load in loads[5:]:
        load.wait()

    def all_sent(sem, chunks):
        where = shared.at[0, pl.ds(0, chunks * chunk)]
        copy(where, where, sem, cr.at[0], twin).wait_send()

    all_sent(ys, ny - 1)
    all_sent(xs, 3 * 6)
    all_sent(vs, 3 * 2)
    all_sent(cs, 4 * ny)
    for i in range(NX):
        arrived(slab(1 - core, -i), cr.at[i])

    for t in range(tiles):
        here = pl.ds(tile_cols[0, 0, t] * 64, 64)
        taken = jnp.concatenate([shared[0, here], shared[1, here]], axis=0)
        prods[t + 1] = jnp.dot(vals[t], taken, preferred_element_type=jnp.float32)

    @pl.loop(0, tiles)
    def _(t):
        prods[t + 1] = prods[t + 1] + prods[links[t]]

    step_rows = 4 * BS
    grads = jnp.zeros((2 * F_IN, HID), jnp.float32)
    for i in range(rows // step_rows):
        here = slice(i * step_rows, (i + 1) * step_rows)
        neigh = jnp.concatenate([prods[links[64 + 4 * i + j]] for j in range(4)], axis=0)
        xn[here, F_IN:] = neigh.astype(jnp.bfloat16)
        pre = jnp.dot(xn[here], w[...], preferred_element_type=jnp.float32) + bias_ref[...]
        sig = jax.nn.sigmoid(pre)
        act[here] = (pre * sig).astype(jnp.bfloat16)
        grad = (gout[here].astype(jnp.float32) * sig * (1.0 + pre * (1.0 - sig))).astype(jnp.bfloat16)
        grads += lax.dot_general(xn[here], grad, (((0,), (0,)), ((), ())), preferred_element_type=jnp.float32)
    for s in range(2):
        for m in range(32):
            r, l = F_IN * s + 8 * (m // 2), 128 * (m % 2)
            part[s, m] = grads[r:r + 8, l:l + 128]

    c = copy(part.at[1 - core], rx_core, ps.at[0], pr.at[0], twin)
    c.start()
    c.wait_recv()
    half[...] = part[core] + rx_core[...]
    plane = [(i, j) for i in range(NX) for j in range(ny) if i or j]
    plane.sort(key=lambda d: -min(d[0], NX - d[0]) - min(d[1], ny - d[1]))
    x_tile = [v * ny for v in xk]
    for i, j in plane:
        copy(half.at[x_tile[i] + yk[j]], rx_xy.at[i * ny + j - 1], ps.at[1], pr.at[1], on(i, j)).start()
    c.wait_send()
    count = NX * ny - 1
    most = rx_xy.at[pl.ds(0, count)]
    copy(most, most, ps.at[1], pr.at[1], twin).wait()
    total = half[x_tile[0] + y]
    for n in range(count):
        total = total + rx_xy[n]
    tile[...] = total
    for k in reversed(ring_order(nz)):
        copy(tile, rx_z.at[z], ps.at[2], pr.at[2], to_z[k]).start()
    rx_z[z] = total
    others = rx_z.at[pl.ds(0, nz - 1)]
    copy(others, others, ps.at[2], pr.at[2], twin).wait()
    total = rx_z[0]
    for k in range(1, nz):
        total = total + rx_z[k]
    nodes = rows * lax.axis_size("blk") * lax.axis_size("grp")
    factor = 1.0 / jnp.sqrt(jnp.float32(nodes))
    own = final.at[core, x_tile[0] + y]
    own[...] = total * factor
    for i, j in plane:
        copy(own, own, fs.at[0], fr.at[0], on(i, j)).start()
    most = final.at[0, pl.ds(0, count)]
    copy(most, most, fs.at[0], fr.at[0], twin).wait()
    c = copy(final.at[core], final.at[core], fs.at[1], fr.at[1], twin)
    c.start()
    c.wait_send()
    copy(final.at[1 - core], final.at[1 - core], fs.at[1], fr.at[1], twin).wait_recv()
    for s, ref in enumerate((gs_ref, gn_ref)):
        for m in range(32):
            ref[8 * (m // 2):8 * (m // 2) + 8, 128 * (m % 2):128 * (m % 2) + 128] = final[s, m]


def store(act, gs, gn, act_out, gs_out, gn_out, sem):
    copies = [
        pltpu.make_async_copy(src, dst, sem.at[i])
        for i, (src, dst) in enumerate(((act, act_out), (gs, gs_out), (gn, gn_out)))
    ]
    for c in copies:
        c.start()
    for c in copies:
        c.wait()


def shards(mesh_shape, features, send_rows, tile_rows, tile_cols, tile_vals, w_self, w_neigh, bias, grad_out):
    rows = features.shape[0]
    tiles = tile_vals.shape[2]
    nx_ylo, rest = mesh_shape
    nyh = 4
    nz = rest // (2 * nyh)
    ny = nyh * YLO
    ndev = nx_ylo * rest
    bf16, f32 = jnp.bfloat16, jnp.float32
    dma = pltpu.SemaphoreType.DMA
    hbm = pl.BlockSpec(memory_space=pltpu.HBM)
    vmem = pl.BlockSpec(memory_space=pltpu.VMEM)
    outs = (
        jax.ShapeDtypeStruct((rows, HID), bf16),
        jax.ShapeDtypeStruct((F_IN, HID), f32),
        jax.ShapeDtypeStruct((F_IN, HID), f32),
    )
    results = pl.pallas_call(
        functools.partial(kernel, (rows, tiles, nz, ny)),
        out_shape=outs,
        in_specs=[hbm] * 9,
        out_specs=(vmem, vmem, vmem),
        scratch_shapes=[
            pltpu.SMEM((1, 1, SEND), jnp.int32),
            pltpu.SMEM((1, 1, tiles), jnp.int32),
            pltpu.SMEM((1, 1, tiles), jnp.int32),
            pltpu.VMEM((1, HID), f32),
            pltpu.VMEM((rows, 2 * F_IN), bf16),
            pltpu.VMEM((2 * F_IN, HID), bf16),
            pltpu.VMEM((tiles, BS, BS), bf16),
            pltpu.VMEM((rows, HID), bf16),
            pltpu.VMEM((nz, SEND, F_IN), f32),
            pltpu.VMEM((SEND, F_IN), f32),
            pltpu.VMEM((2, ndev // 2 * SEND, F_IN), bf16),
            pltpu.VMEM((tiles + 1, BS, F_IN), f32),
            pltpu.SMEM((128,), jnp.int32),
            pltpu.VMEM((2, 32, 8, 128), f32),
            pltpu.VMEM((32, 8, 128), f32),
            pltpu.VMEM((32, 8, 128), f32),
            pltpu.VMEM((NX * ny, 8, 128), f32),
            pltpu.VMEM((8, 128), f32),
            pltpu.VMEM((nz, 8, 128), f32),
            pltpu.VMEM((2, 32, 8, 128), f32),
            dma((9,)), dma, dma, dma, dma((ny,)), dma, dma((NX, ny)), dma, dma((2, NX)), dma, dma((NX,)),
            dma((3,)), dma((3,)), dma((2,)), dma((2,)),
        ],
        compiler_params=pltpu.CompilerParams(
            collective_id=0, has_side_effects=True, vmem_limit_bytes=40 * 1024 * 1024
        ),
    )(*(
        pltpu.with_memory_space_constraint(a, pltpu.HBM)
        for a in (send_rows, tile_rows, tile_cols, features, tile_vals, w_self, w_neigh, bias.reshape(1, HID), grad_out)
    ))
    return pl.pallas_call(
        store,
        out_shape=outs,
        in_specs=[vmem] * 3,
        out_specs=(pl.BlockSpec(memory_space=pl.ANY),) * 3,
        scratch_shapes=[dma((3,))],
    )(*(pltpu.with_memory_space_constraint(r, pltpu.VMEM) for r in results))


def solution(mesh):
    in_specs = (
        P(("blk", "grp"), None),
        P("blk", "grp", None),
        P("blk", "grp", None),
        P("blk", "grp", None),
        P("blk", "grp", None, None, None),
        P(),
        P(),
        P(),
        P(("blk", "grp"), None),
    )
    out_specs = (P(("blk", "grp"), None), P(), P())
    body = functools.partial(shards, (mesh.shape["blk"], mesh.shape["grp"]))
    return jax.shard_map(body, mesh=mesh, in_specs=in_specs, out_specs=out_specs, check_vma=False)
```

```python
import functools

import jax
import jax.numpy as jnp
from jax import lax
from jax.experimental import pallas as pl
from jax.experimental.pallas import tpu as pltpu
from jax.sharding import PartitionSpec as P

MESH = pl.DeviceIdType.MESH
BS = 128
F_IN = 128
HID = 256
SEND = 8
NX = 4
YLO = 2


def ring_order(n):
    return sorted(range(1, n), key=lambda k: (min(k, n - k), k))


def kernel(
    dims,
    send_hbm, trows_hbm, tcols_hbm,
    feat_hbm, vals_hbm, ws_hbm, wn_hbm, bias_hbm, gout_hbm,
    act, gs_ref, gn_ref,
    send_rows, tile_rows, tile_cols, bias_ref, xn, w, vals, gout, zbuf, mine, shared, prods, links,
    part, rx_core, half, rx_xy, tile, rx_z, final,
    load_sem, zs, zr, ys, yr, xs, xr, vs, vr, cs, cr, ps, pr, fs, fr,
):
    rows, tiles, nz, ny = dims
    nyh = ny // YLO
    rb = rows // BS
    chunk = nz * SEND
    blk, grp = lax.axis_index("blk"), lax.axis_index("grp")
    core = grp & 1
    yhi = lax.div(grp, 2 * nz)
    z = (grp >> 1) - yhi * nz
    y = yhi * YLO + (blk & 1)
    x = blk >> 1

    xk = [(x + k) & (NX - 1) for k in range(NX)]
    yk = [(y + k) & (ny - 1) for k in range(ny)]
    zk = [z] + [jnp.where(z + k >= nz, z + k - nz, z + k) for k in range(1, nz)]
    y_grp = [(v >> 1) * (2 * nz) for v in yk]
    y_row = [((v & 1) * nyh + (v >> 1)) * chunk for v in yk]
    x_row = [v * (ny * chunk) for v in xk]
    z_core = 2 * z + core

    def on(i, j):
        return {"blk": xk[i] * YLO + (yk[j] & 1), "grp": y_grp[j] + z_core}

    def copy(src, dst, send, recv, to):
        return pltpu.make_async_remote_copy(
            src_ref=src, dst_ref=dst, send_sem=send, recv_sem=recv, device_id=to, device_id_type=MESH
        )

    to_z = {k: {"blk": blk, "grp": y_grp[0] + 2 * zk[k] + core} for k in range(1, nz)}
    to_y = {k: on(0, k) for k in range(1, ny)}
    to_x = {k: on(k, 0) for k in range(1, NX)}
    twin = {"blk": blk, "grp": grp + 1 - 2 * core}

    barrier = pltpu.get_barrier_semaphore()
    partners = [*(to_z[k] for k in reversed(ring_order(nz))), *to_y.values(), *to_x.values(), twin]
    for partner in partners:
        pl.semaphore_signal(barrier, inc=1, device_id=partner, device_id_type=MESH)

    loads = [
        pltpu.make_async_copy(send_hbm, send_rows, load_sem.at[8]),
        pltpu.make_async_copy(feat_hbm, xn.at[:, pl.ds(0, F_IN)], load_sem.at[0]),
        pltpu.make_async_copy(trows_hbm, tile_rows, load_sem.at[7]),
        pltpu.make_async_copy(vals_hbm.at[0, 0], vals, load_sem.at[1]),
        pltpu.make_async_copy(tcols_hbm, tile_cols, load_sem.at[6]),
        pltpu.make_async_copy(ws_hbm, w.at[pl.ds(0, F_IN)], load_sem.at[3]),
        pltpu.make_async_copy(wn_hbm, w.at[pl.ds(F_IN, F_IN)], load_sem.at[4]),
        pltpu.make_async_copy(bias_hbm, bias_ref, load_sem.at[5]),
        pltpu.make_async_copy(gout_hbm, gout, load_sem.at[2]),
    ]
    for load in loads:
        load.start()
    loads[0].wait()
    loads[1].wait()
    picked = []
    lanes = lax.broadcasted_iota(jnp.int32, (16, F_IN), 0)
    for j in range(SEND):
        row = send_rows[0, 0, j]
        group = xn[pl.ds((row >> 4) * 16, 16), pl.ds(0, F_IN)].astype(jnp.float32)
        picked.append(jnp.sum(jnp.where(lanes == (row & 15), group, 0.0), axis=0, keepdims=True))
    mine[...] = jnp.concatenate(picked, axis=0)

    pl.semaphore_wait(barrier, len(partners))

    for k in reversed(ring_order(nz)):
        copy(mine, zbuf.at[z], zs, zr, to_z[k]).start()
    zbuf[z] = mine[...]

    loads[2].wait()
    loads[3].wait()
    source = lax.broadcasted_iota(jnp.int32, (BS, BS), 0)
    target = lax.broadcasted_iota(jnp.int32, (BS, BS), 1)
    wanted = ((target % 64) // SEND) * (2 * SEND) + (target // 64) * SEND + target % SEND
    order = (source == wanted).astype(jnp.bfloat16)

    @pl.loop(0, tiles // 4)
    def _(i):
        block = vals[pl.ds(i * 4, 4)].reshape(4 * BS, BS)
        moved = jnp.dot(block, order, preferred_element_type=jnp.float32)
        vals[pl.ds(i * 4, 4)] = moved.astype(jnp.bfloat16).reshape(4, BS, BS)

    row_of = [tile_rows[0, 0, t] for t in range(tiles)]

    @pl.loop(0, tiles)
    def _(t):
        own = tile_rows[0, 0, t]
        best = jnp.int32(0)
        for s in range(tiles):
            best = jnp.maximum(best, ((row_of[s] == own) & (s < t)).astype(jnp.int32) * (s + 1))
        links[t] = best

    @pl.loop(0, rb)
    def _(r):
        best = jnp.int32(0)
        for s in range(tiles):
            best = jnp.maximum(best, (row_of[s] == r).astype(jnp.int32) * (s + 1))
        links[64 + r] = best

    prods[0] = jnp.zeros((BS, F_IN), jnp.float32)

    def place(i, j):
        return shared.at[core, pl.ds(pl.multiple_of(x_row[i] + y_row[j], 32), chunk)]

    def slab(core_, i):
        return shared.at[core_, pl.ds(pl.multiple_of(x_row[i], 32), ny * chunk)]

    others = zbuf.at[pl.ds(0, nz - 1)]
    copy(others, others, zs, zr, twin).wait()
    own = place(0, 0)
    own[...] = zbuf[...].reshape(chunk, F_IN).astype(jnp.bfloat16)

    far_y, near_y, all_x = (2, ny - 2, 3, ny - 3, 4), (1, ny - 1), (2, 1, NX - 1)

    def send(where, sems, to):
        copy(where, where, *sems, to).start()

    def arrived(where, recv):
        copy(where, where, cs, recv, twin).wait_recv()

    for i in all_x:
        send(own, (xs, xr.at[i, 0]), to_x[i])
    for k in (*far_y, *near_y):
        send(own, (ys, yr.at[k]), to_y[k])
    for k in far_y[:4]:
        where = place(0, -k)
        arrived(where, yr.at[k])
        for i in all_x:
            send(where, (xs, xr.at[i, k]), to_x[i])
    for i in reversed(all_x):
        where = place(-i, 0)
        arrived(where, xr.at[i, 0])
        for n, k in enumerate(near_y):
            send(where, (vs, vr.at[n, i]), to_y[k])
        send(where, (cs, cr.at[i]), twin)
    for k in far_y[4:]:
        where = place(0, -k)
        arrived(where, yr.at[k])
        for i in all_x:
            send(where, (xs, xr.at[i, k]), to_x[i])
    for k in near_y:
        arrived(place(0, -k), yr.at[k])
    send(slab(core, 0), (cs, cr.at[0]), twin)

    def from_x(k):
        for i in reversed(all_x):
            where = place(-i, -k)
            arrived(where, xr.at[i, k])
            send(where, (cs, cr.at[i]), twin)

    for k in far_y[:2]:
        from_x(k)
    for i in reversed(all_x):
        for n, k in enumerate(near_y):
            where = place(-i, -k)
            arrived(where, vr.at[n, i])
            send(where, (cs, cr.at[i]), twin)
    for k in far_y[2:]:
        from_x(k)
    loads[4].wait()
    for load in loads[5:]:
        load.wait()

    def all_sent(sem, chunks):
        where = shared.at[0, pl.ds(0, chunks * chunk)]
        copy(where, where, sem, cr.at[0], twin).wait_send()

    for i in range(NX):
        arrived(slab(1 - core, -i), cr.at[i])

    for t in range(tiles):
        here = pl.ds(tile_cols[0, 0, t] * 64, 64)
        taken = jnp.concatenate([shared[0, here], shared[1, here]], axis=0)
        prods[t + 1] = jnp.dot(vals[t], taken, preferred_element_type=jnp.float32)

    @pl.loop(0, tiles)
    def _(t):
        prods[t + 1] = prods[t + 1] + prods[links[t]]

    step_rows = 4 * BS
    grads = jnp.zeros((2 * F_IN, HID), jnp.float32)
    for i in range(rows // step_rows):
        here = slice(i * step_rows, (i + 1) * step_rows)
        neigh = jnp.concatenate([prods[links[64 + 4 * i + j]] for j in range(4)], axis=0)
        xn[here, F_IN:] = neigh.astype(jnp.bfloat16)
        pre = jnp.dot(xn[here], w[...], preferred_element_type=jnp.float32) + bias_ref[...]
        sig = jax.nn.sigmoid(pre)
        act[here] = (pre * sig).astype(jnp.bfloat16)
        grad = (gout[here].astype(jnp.float32) * sig * (1.0 + pre * (1.0 - sig))).astype(jnp.bfloat16)
        grads += lax.dot_general(xn[here], grad, (((0,), (0,)), ((), ())), preferred_element_type=jnp.float32)
    for s in range(2):
        for m in range(32):
            r, l = F_IN * s + 8 * (m // 2), 128 * (m % 2)
            part[s, m] = grads[r:r + 8, l:l + 128]

    c = copy(part.at[1 - core], rx_core, ps.at[0], pr.at[0], twin)
    c.start()
    c.wait_recv()
    half[...] = part[core] + rx_core[...]
    plane = [(i, j) for i in range(NX) for j in range(ny) if i or j]
    plane.sort(key=lambda d: -min(d[0], NX - d[0]) - min(d[1], ny - d[1]))
    x_tile = [v * ny for v in xk]
    for i, j in plane:
        copy(half.at[x_tile[i] + yk[j]], rx_xy.at[i * ny + j - 1], ps.at[1], pr.at[1], on(i, j)).start()
    c.wait_send()
    all_sent(ys, ny - 1)
    all_sent(xs, 3 * 6)
    all_sent(vs, 3 * 2)
    all_sent(cs, 4 * ny)
    count = NX * ny - 1
    most = rx_xy.at[pl.ds(0, count)]
    copy(most, most, ps.at[1], pr.at[1], twin).wait()
    total = half[x_tile[0] + y]
    for n in range(count):
        total = total + rx_xy[n]
    tile[...] = total
    for k in reversed(ring_order(nz)):
        copy(tile, rx_z.at[z], ps.at[2], pr.at[2], to_z[k]).start()
    rx_z[z] = total
    others = rx_z.at[pl.ds(0, nz - 1)]
    copy(others, others, ps.at[2], pr.at[2], twin).wait()
    total = rx_z[0]
    for k in range(1, nz):
        total = total + rx_z[k]
    nodes = rows * lax.axis_size("blk") * lax.axis_size("grp")
    factor = 1.0 / jnp.sqrt(jnp.float32(nodes))
    own = final.at[core, x_tile[0] + y]
    own[...] = total * factor
    for i, j in plane:
        copy(own, own, fs.at[0], fr.at[0], on(i, j)).start()
    most = final.at[0, pl.ds(0, count)]
    copy(most, most, fs.at[0], fr.at[0], twin).wait()
    c = copy(final.at[core], final.at[core], fs.at[1], fr.at[1], twin)
    c.start()
    c.wait_send()
    copy(final.at[1 - core], final.at[1 - core], fs.at[1], fr.at[1], twin).wait_recv()
    for s, ref in enumerate((gs_ref, gn_ref)):
        for m in range(32):
            ref[8 * (m // 2):8 * (m // 2) + 8, 128 * (m % 2):128 * (m % 2) + 128] = final[s, m]


def store(act, gs, gn, act_out, gs_out, gn_out, sem):
    copies = [
        pltpu.make_async_copy(src, dst, sem.at[i])
        for i, (src, dst) in enumerate(((act, act_out), (gs, gs_out), (gn, gn_out)))
    ]
    for c in copies:
        c.start()
    for c in copies:
        c.wait()


def shards(mesh_shape, features, send_rows, tile_rows, tile_cols, tile_vals, w_self, w_neigh, bias, grad_out):
    rows = features.shape[0]
    tiles = tile_vals.shape[2]
    nx_ylo, rest = mesh_shape
    nyh = 4
    nz = rest // (2 * nyh)
    ny = nyh * YLO
    ndev = nx_ylo * rest
    bf16, f32 = jnp.bfloat16, jnp.float32
    dma = pltpu.SemaphoreType.DMA
    hbm = pl.BlockSpec(memory_space=pltpu.HBM)
    vmem = pl.BlockSpec(memory_space=pltpu.VMEM)
    outs = (
        jax.ShapeDtypeStruct((rows, HID), bf16),
        jax.ShapeDtypeStruct((F_IN, HID), f32),
        jax.ShapeDtypeStruct((F_IN, HID), f32),
    )
    results = pl.pallas_call(
        functools.partial(kernel, (rows, tiles, nz, ny)),
        out_shape=outs,
        in_specs=[hbm] * 9,
        out_specs=(vmem, vmem, vmem),
        scratch_shapes=[
            pltpu.SMEM((1, 1, SEND), jnp.int32),
            pltpu.SMEM((1, 1, tiles), jnp.int32),
            pltpu.SMEM((1, 1, tiles), jnp.int32),
            pltpu.VMEM((1, HID), f32),
            pltpu.VMEM((rows, 2 * F_IN), bf16),
            pltpu.VMEM((2 * F_IN, HID), bf16),
            pltpu.VMEM((tiles, BS, BS), bf16),
            pltpu.VMEM((rows, HID), bf16),
            pltpu.VMEM((nz, SEND, F_IN), f32),
            pltpu.VMEM((SEND, F_IN), f32),
            pltpu.VMEM((2, ndev // 2 * SEND, F_IN), bf16),
            pltpu.VMEM((tiles + 1, BS, F_IN), f32),
            pltpu.SMEM((128,), jnp.int32),
            pltpu.VMEM((2, 32, 8, 128), f32),
            pltpu.VMEM((32, 8, 128), f32),
            pltpu.VMEM((32, 8, 128), f32),
            pltpu.VMEM((NX * ny, 8, 128), f32),
            pltpu.VMEM((8, 128), f32),
            pltpu.VMEM((nz, 8, 128), f32),
            pltpu.VMEM((2, 32, 8, 128), f32),
            dma((9,)), dma, dma, dma, dma((ny,)), dma, dma((NX, ny)), dma, dma((2, NX)), dma, dma((NX,)),
            dma((3,)), dma((3,)), dma((2,)), dma((2,)),
        ],
        compiler_params=pltpu.CompilerParams(
            collective_id=0, has_side_effects=True, vmem_limit_bytes=40 * 1024 * 1024
        ),
    )(*(
        pltpu.with_memory_space_constraint(a, pltpu.HBM)
        for a in (send_rows, tile_rows, tile_cols, features, tile_vals, w_self, w_neigh, bias.reshape(1, HID), grad_out)
    ))
    return pl.pallas_call(
        store,
        out_shape=outs,
        in_specs=[vmem] * 3,
        out_specs=(pl.BlockSpec(memory_space=pl.ANY),) * 3,
        scratch_shapes=[dma((3,))],
    )(*(pltpu.with_memory_space_constraint(r, pltpu.VMEM) for r in results))


def solution(mesh):
    in_specs = (
        P(("blk", "grp"), None),
        P("blk", "grp", None),
        P("blk", "grp", None),
        P("blk", "grp", None),
        P("blk", "grp", None, None, None),
        P(),
        P(),
        P(),
        P(("blk", "grp"), None),
    )
    out_specs = (P(("blk", "grp"), None), P(), P())
    body = functools.partial(shards, (mesh.shape["blk"], mesh.shape["grp"]))
    return jax.shard_map(body, mesh=mesh, in_specs=in_specs, out_specs=out_specs, check_vma=False)
```

```python
import functools

import jax
import jax.numpy as jnp
from jax import lax
from jax.experimental import pallas as pl
from jax.experimental.pallas import tpu as pltpu
from jax.sharding import PartitionSpec as P

MESH = pl.DeviceIdType.MESH
BS = 128
F_IN = 128
HID = 256
SEND = 8
NX = 4
YLO = 2


def ring_order(n):
    return sorted(range(1, n), key=lambda k: (min(k, n - k), k))


def kernel(
    dims,
    send_hbm, trows_hbm, tcols_hbm,
    feat_hbm, vals_hbm, ws_hbm, wn_hbm, bias_hbm, gout_hbm,
    act, gs_ref, gn_ref,
    send_rows, tile_rows, tile_cols, bias_ref, xn, w, vals, gout, zbuf, mine, shared, prods, links,
    part, rx_core, half, rx_xy, tile, rx_z, final,
    load_sem, zs, zr, ys, yr, xs, xr, vs, vr, cs, cr, ps, pr, fs, fr,
):
    rows, tiles, nz, ny = dims
    nyh = ny // YLO
    rb = rows // BS
    chunk = nz * SEND
    blk, grp = lax.axis_index("blk"), lax.axis_index("grp")
    core = grp & 1
    yhi = lax.div(grp, 2 * nz)
    z = (grp >> 1) - yhi * nz
    y = yhi * YLO + (blk & 1)
    x = blk >> 1

    xk = [(x + k) & (NX - 1) for k in range(NX)]
    yk = [(y + k) & (ny - 1) for k in range(ny)]
    zk = [z] + [jnp.where(z + k >= nz, z + k - nz, z + k) for k in range(1, nz)]
    y_grp = [(v >> 1) * (2 * nz) for v in yk]
    y_row = [((v & 1) * nyh + (v >> 1)) * chunk for v in yk]
    x_row = [v * (ny * chunk) for v in xk]
    z_core = 2 * z + core

    def on(i, j):
        return {"blk": xk[i] * YLO + (yk[j] & 1), "grp": y_grp[j] + z_core}

    def copy(src, dst, send, recv, to):
        return pltpu.make_async_remote_copy(
            src_ref=src, dst_ref=dst, send_sem=send, recv_sem=recv, device_id=to, device_id_type=MESH
        )

    to_z = {k: {"blk": blk, "grp": y_grp[0] + 2 * zk[k] + core} for k in range(1, nz)}
    to_y = {k: on(0, k) for k in range(1, ny)}
    to_x = {k: on(k, 0) for k in range(1, NX)}
    twin = {"blk": blk, "grp": grp + 1 - 2 * core}

    barrier = pltpu.get_barrier_semaphore()
    partners = [*(to_z[k] for k in reversed(ring_order(nz))), *to_y.values(), *to_x.values(), twin]
    for partner in partners:
        pl.semaphore_signal(barrier, inc=1, device_id=partner, device_id_type=MESH)

    loads = [
        pltpu.make_async_copy(send_hbm, send_rows, load_sem.at[8]),
        pltpu.make_async_copy(feat_hbm, xn.at[:, pl.ds(0, F_IN)], load_sem.at[0]),
        pltpu.make_async_copy(trows_hbm, tile_rows, load_sem.at[7]),
        pltpu.make_async_copy(vals_hbm.at[0, 0], vals, load_sem.at[1]),
        pltpu.make_async_copy(tcols_hbm, tile_cols, load_sem.at[6]),
        pltpu.make_async_copy(ws_hbm, w.at[pl.ds(0, F_IN)], load_sem.at[3]),
        pltpu.make_async_copy(wn_hbm, w.at[pl.ds(F_IN, F_IN)], load_sem.at[4]),
        pltpu.make_async_copy(bias_hbm, bias_ref, load_sem.at[5]),
        pltpu.make_async_copy(gout_hbm, gout, load_sem.at[2]),
    ]
    for load in loads:
        load.start()
    loads[0].wait()
    loads[1].wait()
    picked = []
    lanes = lax.broadcasted_iota(jnp.int32, (16, F_IN), 0)
    for j in range(SEND):
        row = send_rows[0, 0, j]
        group = xn[pl.ds((row >> 4) * 16, 16), pl.ds(0, F_IN)].astype(jnp.float32)
        picked.append(jnp.sum(jnp.where(lanes == (row & 15), group, 0.0), axis=0, keepdims=True))
    mine[...] = jnp.concatenate(picked, axis=0)

    pl.semaphore_wait(barrier, len(partners))

    for k in reversed(ring_order(nz)):
        copy(mine, zbuf.at[z], zs, zr, to_z[k]).start()
    zbuf[z] = mine[...]

    loads[2].wait()
    loads[3].wait()
    source = lax.broadcasted_iota(jnp.int32, (BS, BS), 0)
    target = lax.broadcasted_iota(jnp.int32, (BS, BS), 1)
    wanted = ((target % 64) // SEND) * (2 * SEND) + (target // 64) * SEND + target % SEND
    order = (source == wanted).astype(jnp.bfloat16)

    @pl.loop(0, tiles // 4)
    def _(i):
        block = vals[pl.ds(i * 4, 4)].reshape(4 * BS, BS)
        moved = jnp.dot(block, order, preferred_element_type=jnp.float32)
        vals[pl.ds(i * 4, 4)] = moved.astype(jnp.bfloat16).reshape(4, BS, BS)

    row_of = [tile_rows[0, 0, t] for t in range(tiles)]

    @pl.loop(0, tiles)
    def _(t):
        own = tile_rows[0, 0, t]
        best = jnp.int32(0)
        for s in range(tiles):
            best = jnp.maximum(best, ((row_of[s] == own) & (s < t)).astype(jnp.int32) * (s + 1))
        links[t] = best

    @pl.loop(0, rb)
    def _(r):
        best = jnp.int32(0)
        for s in range(tiles):
            best = jnp.maximum(best, (row_of[s] == r).astype(jnp.int32) * (s + 1))
        links[64 + r] = best

    prods[0] = jnp.zeros((BS, F_IN), jnp.float32)

    def place(i, j):
        return shared.at[core, pl.ds(pl.multiple_of(x_row[i] + y_row[j], 32), chunk)]

    def slab(core_, i):
        return shared.at[core_, pl.ds(pl.multiple_of(x_row[i], 32), ny * chunk)]

    others = zbuf.at[pl.ds(0, nz - 1)]
    copy(others, others, zs, zr, twin).wait()
    own = place(0, 0)
    own[...] = zbuf[...].reshape(chunk, F_IN).astype(jnp.bfloat16)

    far_y, near_y, all_x = (2, ny - 2, 3, ny - 3, 4), (1, ny - 1), (2, 1, NX - 1)

    def send(where, sems, to):
        copy(where, where, *sems, to).start()

    def arrived(where, recv):
        copy(where, where, cs, recv, twin).wait_recv()

    for i in all_x:
        send(own, (xs, xr.at[i, 0]), to_x[i])
    for k in (*far_y, *near_y):
        send(own, (ys, yr.at[k]), to_y[k])
    for k in far_y[:4]:
        where = place(0, -k)
        arrived(where, yr.at[k])
        for i in all_x:
            send(where, (xs, xr.at[i, k]), to_x[i])
    for i in reversed(all_x):
        where = place(-i, 0)
        arrived(where, xr.at[i, 0])
        for n, k in enumerate(near_y):
            send(where, (vs, vr.at[n, i]), to_y[k])
        send(where, (cs, cr.at[i]), twin)
    for k in far_y[4:]:
        where = place(0, -k)
        arrived(where, yr.at[k])
        for i in all_x:
            send(where, (xs, xr.at[i, k]), to_x[i])
    for k in near_y:
        arrived(place(0, -k), yr.at[k])
    send(slab(core, 0), (cs, cr.at[0]), twin)

    def from_x(k):
        for i in reversed(all_x):
            where = place(-i, -k)
            arrived(where, xr.at[i, k])
            send(where, (cs, cr.at[i]), twin)

    for k in far_y[:2]:
        from_x(k)
    for i in reversed(all_x):
        for n, k in enumerate(near_y):
            where = place(-i, -k)
            arrived(where, vr.at[n, i])
            send(where, (cs, cr.at[i]), twin)
    for k in far_y[2:]:
        from_x(k)
    loads[4].wait()
    for load in loads[5:]:
        load.wait()

    def all_sent(sem, chunks):
        where = shared.at[0, pl.ds(0, chunks * chunk)]
        copy(where, where, sem, cr.at[0], twin).wait_send()

    for i in range(NX):
        arrived(slab(1 - core, -i), cr.at[i])

    for t in range(tiles):
        here = pl.ds(tile_cols[0, 0, t] * 64, 64)
        taken = jnp.concatenate([shared[0, here], shared[1, here]], axis=0)
        prods[t + 1] = jnp.dot(vals[t], taken, preferred_element_type=jnp.float32) + prods[links[t]]

    step_rows = 4 * BS
    grads = jnp.zeros((2 * F_IN, HID), jnp.float32)
    for i in range(rows // step_rows):
        here = slice(i * step_rows, (i + 1) * step_rows)
        neigh = jnp.concatenate([prods[links[64 + 4 * i + j]] for j in range(4)], axis=0)
        xn[here, F_IN:] = neigh.astype(jnp.bfloat16)
        pre = jnp.dot(xn[here], w[...], preferred_element_type=jnp.float32) + bias_ref[...]
        sig = jax.nn.sigmoid(pre)
        act[here] = (pre * sig).astype(jnp.bfloat16)
        grad = (gout[here].astype(jnp.float32) * sig * (1.0 + pre * (1.0 - sig))).astype(jnp.bfloat16)
        grads += lax.dot_general(xn[here], grad, (((0,), (0,)), ((), ())), preferred_element_type=jnp.float32)
    for s in range(2):
        for m in range(32):
            r, l = F_IN * s + 8 * (m // 2), 128 * (m % 2)
            part[s, m] = grads[r:r + 8, l:l + 128]

    c = copy(part.at[1 - core], rx_core, ps.at[0], pr.at[0], twin)
    c.start()
    c.wait_recv()
    half[...] = part[core] + rx_core[...]
    plane = [(i, j) for i in range(NX) for j in range(ny) if i or j]
    plane.sort(key=lambda d: -min(d[0], NX - d[0]) - min(d[1], ny - d[1]))
    x_tile = [v * ny for v in xk]
    for i, j in plane:
        copy(half.at[x_tile[i] + yk[j]], rx_xy.at[i * ny + j - 1], ps.at[1], pr.at[1], on(i, j)).start()
    c.wait_send()
    all_sent(ys, ny - 1)
    all_sent(xs, 3 * 6)
    all_sent(vs, 3 * 2)
    all_sent(cs, 4 * ny)
    count = NX * ny - 1
    most = rx_xy.at[pl.ds(0, count)]
    copy(most, most, ps.at[1], pr.at[1], twin).wait()
    total = half[x_tile[0] + y]
    for n in range(count):
        total = total + rx_xy[n]
    tile[...] = total
    for k in reversed(ring_order(nz)):
        copy(tile, rx_z.at[z], ps.at[2], pr.at[2], to_z[k]).start()
    rx_z[z] = total
    others = rx_z.at[pl.ds(0, nz - 1)]
    copy(others, others, ps.at[2], pr.at[2], twin).wait()
    total = rx_z[0]
    for k in range(1, nz):
        total = total + rx_z[k]
    nodes = rows * lax.axis_size("blk") * lax.axis_size("grp")
    factor = 1.0 / jnp.sqrt(jnp.float32(nodes))
    own = final.at[core, x_tile[0] + y]
    own[...] = total * factor
    for i, j in plane:
        copy(own, own, fs.at[0], fr.at[0], on(i, j)).start()
    most = final.at[0, pl.ds(0, count)]
    copy(most, most, fs.at[0], fr.at[0], twin).wait()
    c = copy(final.at[core], final.at[core], fs.at[1], fr.at[1], twin)
    c.start()
    c.wait_send()
    copy(final.at[1 - core], final.at[1 - core], fs.at[1], fr.at[1], twin).wait_recv()
    for s, ref in enumerate((gs_ref, gn_ref)):
        for m in range(32):
            ref[8 * (m // 2):8 * (m // 2) + 8, 128 * (m % 2):128 * (m % 2) + 128] = final[s, m]


def store(act, gs, gn, act_out, gs_out, gn_out, sem):
    copies = [
        pltpu.make_async_copy(src, dst, sem.at[i])
        for i, (src, dst) in enumerate(((act, act_out), (gs, gs_out), (gn, gn_out)))
    ]
    for c in copies:
        c.start()
    for c in copies:
        c.wait()


def shards(mesh_shape, features, send_rows, tile_rows, tile_cols, tile_vals, w_self, w_neigh, bias, grad_out):
    rows = features.shape[0]
    tiles = tile_vals.shape[2]
    nx_ylo, rest = mesh_shape
    nyh = 4
    nz = rest // (2 * nyh)
    ny = nyh * YLO
    ndev = nx_ylo * rest
    bf16, f32 = jnp.bfloat16, jnp.float32
    dma = pltpu.SemaphoreType.DMA
    hbm = pl.BlockSpec(memory_space=pltpu.HBM)
    vmem = pl.BlockSpec(memory_space=pltpu.VMEM)
    outs = (
        jax.ShapeDtypeStruct((rows, HID), bf16),
        jax.ShapeDtypeStruct((F_IN, HID), f32),
        jax.ShapeDtypeStruct((F_IN, HID), f32),
    )
    results = pl.pallas_call(
        functools.partial(kernel, (rows, tiles, nz, ny)),
        out_shape=outs,
        in_specs=[hbm] * 9,
        out_specs=(vmem, vmem, vmem),
        scratch_shapes=[
            pltpu.SMEM((1, 1, SEND), jnp.int32),
            pltpu.SMEM((1, 1, tiles), jnp.int32),
            pltpu.SMEM((1, 1, tiles), jnp.int32),
            pltpu.VMEM((1, HID), f32),
            pltpu.VMEM((rows, 2 * F_IN), bf16),
            pltpu.VMEM((2 * F_IN, HID), bf16),
            pltpu.VMEM((tiles, BS, BS), bf16),
            pltpu.VMEM((rows, HID), bf16),
            pltpu.VMEM((nz, SEND, F_IN), f32),
            pltpu.VMEM((SEND, F_IN), f32),
            pltpu.VMEM((2, ndev // 2 * SEND, F_IN), bf16),
            pltpu.VMEM((tiles + 1, BS, F_IN), f32),
            pltpu.SMEM((128,), jnp.int32),
            pltpu.VMEM((2, 32, 8, 128), f32),
            pltpu.VMEM((32, 8, 128), f32),
            pltpu.VMEM((32, 8, 128), f32),
            pltpu.VMEM((NX * ny, 8, 128), f32),
            pltpu.VMEM((8, 128), f32),
            pltpu.VMEM((nz, 8, 128), f32),
            pltpu.VMEM((2, 32, 8, 128), f32),
            dma((9,)), dma, dma, dma, dma((ny,)), dma, dma((NX, ny)), dma, dma((2, NX)), dma, dma((NX,)),
            dma((3,)), dma((3,)), dma((2,)), dma((2,)),
        ],
        compiler_params=pltpu.CompilerParams(
            collective_id=0, has_side_effects=True, vmem_limit_bytes=40 * 1024 * 1024
        ),
    )(*(
        pltpu.with_memory_space_constraint(a, pltpu.HBM)
        for a in (send_rows, tile_rows, tile_cols, features, tile_vals, w_self, w_neigh, bias.reshape(1, HID), grad_out)
    ))
    return pl.pallas_call(
        store,
        out_shape=outs,
        in_specs=[vmem] * 3,
        out_specs=(pl.BlockSpec(memory_space=pl.ANY),) * 3,
        scratch_shapes=[dma((3,))],
    )(*(pltpu.with_memory_space_constraint(r, pltpu.VMEM) for r in results))


def solution(mesh):
    in_specs = (
        P(("blk", "grp"), None),
        P("blk", "grp", None),
        P("blk", "grp", None),
        P("blk", "grp", None),
        P("blk", "grp", None, None, None),
        P(),
        P(),
        P(),
        P(("blk", "grp"), None),
    )
    out_specs = (P(("blk", "grp"), None), P(), P())
    body = functools.partial(shards, (mesh.shape["blk"], mesh.shape["grp"]))
    return jax.shard_map(body, mesh=mesh, in_specs=in_specs, out_specs=out_specs, check_vma=False)
```
